512 devices in a mesh: dp: 16 (over z_hi, y, core), loop: 32 (over z_lo, x).
Axes of the slice: x: 4, y: 4, z: 16 (z_hi: 2, z_lo: 8; z = z_hi * 8 + z_lo), core: 2. Of those that a mesh axis runs over, the one named last changes fastest.
Arguments:
- image_embeds: bfloat16 [65536, 1152], P(('dp', 'loop')), may hold values from -0.6 to 0.6
- text_embeds: bfloat16 [65536, 1152], P(('dp', 'loop')), may hold values from -0.6 to 0.6
- log_scale: float32 [1], replicated, may hold values from 2 to 2.7
- logit_bias: float32 [1], replicated, may hold values from -8 to -5
Outputs:
- loss: float32 [1], replicated
- image_grad: bfloat16 [65536, 1152], P(('dp', 'loop'))
- text_grad: bfloat16 [65536, 1152], P(('dp', 'loop'))
- grad_log_scale: float32 [1], replicated
- grad_bias: float32 [1], replicated
The draws below stay inside these ranges and needn't reach their ends.
All inputs are finite; a program needn't handle non-finite values.
Results may differ from the reference program's by a relative error of at most 0.0065.
Values may be sent and summed in bfloat16 or wider, within the bound.
No kernel may reach another device: no remote copies, remote signals or barrier semaphores. Data moves between devices by JAX's collectives and lax.ppermute only.
A program may use at most 64 MiB of HBM per device.

```python
import math
import jax
import jax.numpy as jnp
from jax import lax

D = 1152
ROWS_DEV = 128
GROUP = 2048
BATCH = 65536
N_DP = 16
N_LOOP = 32


def shared_rows(key):
    key = jax.random.fold_in(key, 11)
    keys = jax.random.split(key, 3)
    clusters = max(GROUP // 8, 1)
    members = jax.random.randint(keys[0], (BATCH,), 0, clusters)
    centers = jnp.clip(jax.random.normal(keys[1], (clusters, D), jnp.float32), -4.0, 4.0)
    single = jnp.clip(jax.random.normal(keys[2], (BATCH, D), jnp.float32), -4.0, 4.0)
    return 0.5 * jnp.take(centers, members, axis=0) + 0.59 * single


def draw_image_embeds(key, part):
    base = shared_rows(key)
    key = jax.random.fold_in(key, 3)
    noise_key, scale_key = jax.random.split(key)
    noise = jnp.clip(jax.random.normal(noise_key, (BATCH, D), jnp.float32), -4.0, 4.0)
    scales = jnp.exp(jax.random.uniform(scale_key, (BATCH, 1), jnp.float32, math.log(0.02), math.log(0.05)))
    return (scales * (base + 0.63 * noise)).astype(jnp.bfloat16)


def draw_text_embeds(key, part):
    base = shared_rows(key)
    key = jax.random.fold_in(key, 5)
    noise_key, scale_key = jax.random.split(key)
    noise = jnp.clip(jax.random.normal(noise_key, (BATCH, D), jnp.float32), -4.0, 4.0)
    scales = jnp.exp(jax.random.uniform(scale_key, (BATCH, 1), jnp.float32, math.log(0.02), math.log(0.05)))
    return (scales * (base + 0.63 * noise)).astype(jnp.bfloat16)


def setup_inputs(seed: int = 0) -> dict:
    splits = jax.random.split(jax.random.key(seed), 5)
    return {
        "image_embeds": draw_image_embeds(jax.random.fold_in(splits[4], 71), 0),
        "text_embeds": draw_text_embeds(jax.random.fold_in(splits[4], 71), 0),
        "log_scale": jnp.clip(jax.random.uniform(splits[2], (1,), jnp.float32, 2.0, 2.7), 2.0, 2.7),
        "logit_bias": jnp.clip(jax.random.uniform(splits[3], (1,), jnp.float32, -8.0, -5.0), -8.0, -5.0),
    }


EPSILON = 1e-06

def unit_rows(matrix):
    floats = matrix.astype(jnp.float32)
    return floats * lax.rsqrt(lax.optimization_barrier(jnp.sum(floats * floats, axis=1, keepdims=True)) + EPSILON)

def unit_pull(matrix, cotangent):
    _, pullback = jax.vjp(unit_rows, matrix.astype(jnp.float32))
    return pullback(cotangent)[0]

def rounded(values):
    return lax.optimization_barrier(values.astype(jnp.bfloat16)).astype(jnp.float32)

def to_groups(matrix):
    return matrix.reshape(N_DP, N_LOOP, ROWS_DEV, D).transpose(1, 0, 2, 3).reshape(N_LOOP, N_DP * ROWS_DEV, D)

def from_groups(matrix):
    return matrix.reshape(N_LOOP, N_DP, ROWS_DEV, D).transpose(1, 0, 2, 3).reshape(BATCH, D)

def reference(image_embeds, text_embeds, log_scale, logit_bias):
    temper = jnp.exp(log_scale[0])
    offset = logit_bias[0]
    image_groups = to_groups(unit_rows(image_embeds).astype(jnp.bfloat16).astype(jnp.float32))
    text_groups = to_groups(unit_rows(text_embeds).astype(jnp.bfloat16).astype(jnp.float32))
    member_ids = jnp.arange(N_DP * ROWS_DEV, dtype=jnp.int32)
    positive = member_ids[:, None] == member_ids[None, :]
    signs = jnp.where(positive, jnp.float32(-1.0), jnp.float32(1.0))

    def group_step(carry, group):
        loss_acc, scale_acc, bias_acc = carry
        images_here = lax.dynamic_index_in_dim(image_groups, group, 0, keepdims=False)
        texts_here = lax.dynamic_index_in_dim(text_groups, group, 0, keepdims=False)
        scaled = temper * jnp.einsum('ad,cd->ac', images_here, texts_here)
        logits = scaled + offset
        losses = jax.nn.softplus(signs * logits)
        coef = jax.nn.sigmoid(logits) - positive.astype(jnp.float32)
        coef_half = rounded(coef)
        image_term = temper * jnp.einsum('ac,cd->ad', coef_half, texts_here)
        text_term = temper * jnp.einsum('ac,ad->cd', coef_half, images_here)
        new_carry = (loss_acc + jnp.sum(losses), scale_acc + jnp.sum(coef * scaled), bias_acc + jnp.sum(coef))
        return (new_carry, (image_term, text_term))
    start = (jnp.zeros((), jnp.float32), jnp.zeros((), jnp.float32), jnp.zeros((), jnp.float32))
    groups = jnp.arange(N_LOOP, dtype=jnp.int32)
    final, terms = lax.scan(group_step, start, groups)
    loss_acc, scale_acc, bias_acc = final
    image_cot = from_groups(terms[0])
    text_cot = from_groups(terms[1])
    image_grad = unit_pull(image_embeds, image_cot).astype(jnp.bfloat16)
    text_grad = unit_pull(text_embeds, text_cot).astype(jnp.bfloat16)
    loss = jnp.reshape(loss_acc / BATCH, (1,))
    return (loss, image_grad, text_grad, jnp.reshape(scale_acc, (1,)), jnp.reshape(bias_acc, (1,)))
```

```python
import jax
import jax.numpy as jnp
from jax import lax
from jax.experimental import pallas as pl
from jax.experimental.pallas import tpu as pltpu
from jax.sharding import Mesh, PartitionSpec as P

EPSILON = 1e-06
F32 = jnp.float32
BF16 = jnp.bfloat16
AXES = ("zh", "y", "c", "zl", "x")
SIZES = (2, 4, 2, 8, 4)

VMEM = pl.BlockSpec(memory_space=pltpu.VMEM)
SMEM = pl.BlockSpec(memory_space=pltpu.SMEM)
PARAMS = pltpu.CompilerParams(vmem_limit_bytes=40 * 1024 * 1024)
SWAP = ((0, 1), (1, 0))
CHUNK = 256


def call(kernel, outs, in_specs, args):
    return pl.pallas_call(
        kernel,
        out_shape=[jax.ShapeDtypeStruct(shape, dtype) for shape, dtype in outs],
        in_specs=in_specs,
        out_specs=[VMEM] * len(outs),
        compiler_params=PARAMS,
    )(*args)


def unit(matrix):
    floats = matrix.astype(F32)
    return (floats * lax.rsqrt(jnp.sum(floats * floats, axis=1, keepdims=True) + EPSILON)).astype(BF16)


def norm_kernel(image_ref, text_ref, image_out, text_out):
    image_out[...] = unit(image_ref[...])
    text = unit(text_ref[...])
    for k in range(text_out.shape[0]):
        text_out[k] = text


def fold(values):
    rows, cols = values.shape
    total = jnp.sum(values.reshape(rows // 8, 8, cols), axis=0)
    return sum(total[:, k * 128 : (k + 1) * 128] for k in range(cols // 128))


def pair_chunk(image, text, temper, offset, positive):
    products = lax.dot_general(image, text, (((1,), (1,)), ((), ())), preferred_element_type=F32)
    scaled = temper * products
    logits = scaled + offset
    small = jnp.exp(-jnp.abs(logits))
    part = 1.0 / (1.0 + small)
    coef = jnp.where(logits >= 0.0, 1.0, small) * part
    signed = logits
    if positive is not None:
        coef = coef - jnp.where(positive, 1.0, 0.0)
        signed = jnp.where(positive, -logits, logits)
    losses = jnp.maximum(signed, 0.0) + jnp.log1p(small)
    return coef, (fold(losses), fold(coef * scaled), fold(coef))


def rows_of(ref, chunk):
    per = CHUNK // 128
    return ref[chunk * per : (chunk + 1) * per].reshape(CHUNK, ref.shape[2])


def pairs(scale_ref, bias_ref, image, mine_ref, sib_ref, coef_mine, coef_sib, y=None):
    temper = jnp.exp(jnp.full((1, CHUNK), scale_ref[0], F32))
    offset = bias_ref[0]
    sums, cot = None, None
    for ref, out in ((mine_ref, coef_mine), (sib_ref, coef_sib)):
        for chunk in range(ref.shape[0] * 128 // CHUNK):
            text = rows_of(ref, chunk)
            positive = None
            if y is not None and ref is mine_ref:
                rows = lax.broadcasted_iota(jnp.int32, (128, CHUNK), 0)
                cols = lax.broadcasted_iota(jnp.int32, (128, CHUNK), 1)
                positive = cols + chunk * CHUNK == rows + y * 128
            coef, terms = pair_chunk(image, text, temper, offset, positive)
            half = coef.astype(BF16)
            out[:, chunk * CHUNK : (chunk + 1) * CHUNK] = half
            part = jnp.dot(half, text, preferred_element_type=F32)
            cot = part if cot is None else cot + part
            sums = terms if sums is None else tuple(a + b for a, b in zip(sums, terms))
    return cot, sums


def own_kernel(scale_ref, bias_ref, y_ref, image_ref, mine_ref, sib_ref, coef_mine, coef_sib, cot_ref, sums_ref):
    cot, sums = pairs(
        scale_ref, bias_ref, image_ref[...], mine_ref, sib_ref, coef_mine, coef_sib, y_ref[0]
    )
    cot_ref[...] = cot
    for k in range(3):
        sums_ref[k] = sums[k]


def cross_kernel(scale_ref, bias_ref, image_ref, mine_ref, sib_ref, before_ref, coef_mine, coef_sib, cot_ref, sums_ref):
    cot, sums = pairs(scale_ref, bias_ref, image_ref[...], mine_ref, sib_ref, coef_mine, coef_sib)
    cot_ref[...] = cot.astype(BF16)
    sums_ref[...] = jnp.zeros_like(sums_ref)
    for k in range(3):
        sums_ref[k : k + 1, :] = jnp.sum(sums[k] + before_ref[k], axis=0, keepdims=True)


def text_part(own_ref, cross_ref, image_ref, image_far_ref, k):
    cols = slice(k * 128, (k + 1) * 128)
    dims = (((0,), (0,)), ((), ()))
    return lax.dot_general(own_ref[:, cols], image_ref[...], dims, preferred_element_type=F32) + lax.dot_general(
        cross_ref[:, cols], image_far_ref[...], dims, preferred_element_type=F32
    )


def text_sib_kernel(own_ref, cross_ref, image_ref, image_far_ref, out_ref):
    for k in range(out_ref.shape[0]):
        out_ref[k] = text_part(own_ref, cross_ref, image_ref, image_far_ref, k).astype(BF16)


def text_mine_kernel(y_ref, own_ref, cross_ref, image_ref, image_far_ref, got_ref, out_ref, kept_ref):
    for k in range(out_ref.shape[0]):
        total = text_part(own_ref, cross_ref, image_ref, image_far_ref, k) + got_ref[k].astype(F32)
        out_ref[k] = total.astype(BF16)

        @pl.when(y_ref[0] == k)
        def _():
            kept_ref[...] = total


def pull(embeds, cot, scale):
    floats = embeds.astype(F32)
    cot = jnp.exp(jnp.full((1, floats.shape[1]), scale, F32)) * cot
    inverse = lax.rsqrt(jnp.sum(floats * floats, axis=1, keepdims=True) + EPSILON)
    along = jnp.sum(cot * floats, axis=1, keepdims=True)
    return (inverse * cot - (inverse * inverse * inverse * along) * floats).astype(BF16)


def image_kernel(scale_ref, embeds_ref, cot_ref, got_ref, out_ref):
    out_ref[...] = pull(embeds_ref[...], cot_ref[...] + got_ref[...].astype(F32), scale_ref[0])


def text_kernel(scale_ref, y_ref, embeds_ref, kept_ref, got_ref, out_ref):
    total = kept_ref[...]
    for k in range(got_ref.shape[0]):
        total = total + jnp.where(y_ref[0] == k, 0.0, got_ref[k].astype(F32))
    out_ref[...] = pull(embeds_ref[...], total, scale_ref[0])


def everyone(values, axes):
    count = lax.axis_size(axes)
    spread = jnp.broadcast_to(values[None], (count,) + values.shape)
    return jnp.sum(lax.all_to_all(spread, axes, 0, 0, tiled=True), axis=0)


def on_device(image_embeds, text_embeds, log_scale, logit_bias):
    rows, width = image_embeds.shape
    y_count = lax.axis_size("y")
    y = jnp.reshape(lax.axis_index("y"), (1,))
    block, blocks = (rows, width), (y_count, rows, width)
    half = (rows, y_count * rows)

    image, text = call(norm_kernel, [(block, BF16), (blocks, BF16)], [VMEM] * 2, (image_embeds, text_embeds))
    image_far = lax.ppermute(image, "zh", SWAP)
    mine = lax.all_to_all(text, "y", 0, 0, tiled=True)
    sib = lax.ppermute(mine, "c", SWAP)

    own_mine, own_sib, image_cot, sums = call(
        own_kernel,
        [(half, BF16), (half, BF16), (block, F32), ((3, 8, 128), F32)],
        [SMEM] * 3 + [VMEM] * 3,
        (log_scale, logit_bias, y, image, mine, sib),
    )
    far_mine, far_sib, far_cot, sums = call(
        cross_kernel,
        [(half, BF16), (half, BF16), (block, BF16), ((8, 128), F32)],
        [SMEM] * 2 + [VMEM] * 4,
        (log_scale, logit_bias, image_far, mine, sib, sums),
    )
    far_got = lax.ppermute(far_cot, "zh", SWAP)

    (text_sib,) = call(text_sib_kernel, [(blocks, BF16)], [VMEM] * 4, (own_sib, far_sib, image, image_far))
    text_got = lax.ppermute(text_sib, "c", SWAP)
    text_send, text_kept = call(
        text_mine_kernel,
        [(blocks, BF16), (block, F32)],
        [SMEM] + [VMEM] * 5,
        (y, own_mine, far_mine, image, image_far, text_got),
    )
    text_parts = lax.all_to_all(text_send, "y", 0, 0, tiled=True)

    totals = everyone(everyone(sums, ("y", "c", "x")), ("zh", "zl"))
    totals = jnp.sum(totals[:3], axis=1)

    (text_grad,) = call(
        text_kernel, [(block, BF16)], [SMEM] * 2 + [VMEM] * 3, (log_scale, y, text_embeds, text_kept, text_parts)
    )
    (image_grad,) = call(
        image_kernel, [(block, BF16)], [SMEM] + [VMEM] * 3, (log_scale, image_embeds, image_cot, far_got)
    )
    batch = rows * lax.axis_size(AXES)
    return totals[0:1] / batch, image_grad, text_grad, totals[1:2], totals[2:3]


def solution(mesh):
    fine = Mesh(mesh.devices.reshape(SIZES), AXES)
    return jax.shard_map(
        on_device,
        mesh=fine,
        in_specs=(P(AXES, None), P(AXES, None), P(), P()),
        out_specs=(P(), P(AXES, None), P(AXES, None), P(), P()),
        check_vma=False,
    )
```

```python
import jax
import jax.numpy as jnp
from jax import lax
from jax.experimental import pallas as pl
from jax.experimental.pallas import tpu as pltpu
from jax.sharding import Mesh, PartitionSpec as P

EPSILON = 1e-06
F32 = jnp.float32
BF16 = jnp.bfloat16
AXES = ("zh", "y", "c", "zl", "x")
SIZES = (2, 4, 2, 8, 4)

VMEM = pl.BlockSpec(memory_space=pltpu.VMEM)
SMEM = pl.BlockSpec(memory_space=pltpu.SMEM)
HBM = pl.BlockSpec(memory_space=pltpu.HBM)
PARAMS = pltpu.CompilerParams(vmem_limit_bytes=16 * 1024 * 1024)
SWAP = ((0, 1), (1, 0))
CHUNK = 256
EXTRA = 16


def call(kernel, outs, in_specs, args, scratch=(), out_specs=None):
    return pl.pallas_call(
        kernel,
        out_shape=[jax.ShapeDtypeStruct(shape, dtype) for shape, dtype in outs],
        in_specs=in_specs,
        out_specs=out_specs or [VMEM] * len(outs),
        scratch_shapes=scratch,
        compiler_params=PARAMS,
    )(*args)


def unit(matrix):
    floats = matrix.astype(F32)
    return (floats * lax.rsqrt(jnp.sum(floats * floats, axis=1, keepdims=True) + EPSILON)).astype(BF16)


def norm_kernel(image_ref, text_ref, image_out, text_out, image_in, text_in, sems):
    copies = [
        pltpu.make_async_copy(image_ref, image_in, sems.at[0]),
        pltpu.make_async_copy(text_ref, text_in, sems.at[1]),
    ]
    for copy in copies:
        copy.start()
    copies[0].wait()
    image_out[...] = unit(image_in[...])
    copies[1].wait()
    text = unit(text_in[...])
    for k in range(text_out.shape[0]):
        text_out[k] = text


def fold(values):
    rows, cols = values.shape
    total = jnp.sum(values.reshape(rows // 8, 8, cols), axis=0)
    return sum(total[:, k * 128 : (k + 1) * 128] for k in range(cols // 128))


def pair_chunk(image, text, temper, offset, positive):
    products = lax.dot_general(image, text, (((1,), (1,)), ((), ())), preferred_element_type=F32)
    scaled = temper * products
    logits = scaled + offset
    small = jnp.exp(-jnp.abs(logits))
    part = 1.0 / (1.0 + small)
    coef = jnp.where(logits >= 0.0, 1.0, small) * part
    signed = logits
    if positive is not None:
        coef = coef - jnp.where(positive, 1.0, 0.0)
        signed = jnp.where(positive, -logits, logits)
    losses = jnp.maximum(signed, 0.0) + jnp.log1p(small)
    return coef, (fold(losses), fold(coef * scaled), fold(coef))


def pairs(scale_ref, bias_ref, image, mine_ref, sib_ref, coef_mine, coef_sib, y=None):
    per = CHUNK // 128
    temper = jnp.exp(jnp.full((1, CHUNK), scale_ref[0], F32))
    offset = bias_ref[0]
    sums, cot = None, None
    for ref, out in ((mine_ref, coef_mine), (sib_ref, coef_sib)):
        for first in range(0, ref.shape[0], per):
            text = ref[first : first + per].reshape(CHUNK, ref.shape[2])
            positive = None
            if y is not None and ref is mine_ref:
                rows = lax.broadcasted_iota(jnp.int32, (128, CHUNK), 0)
                cols = lax.broadcasted_iota(jnp.int32, (128, CHUNK), 1)
                positive = cols + first * 128 == rows + y * 128
            coef, terms = pair_chunk(image, text, temper, offset, positive)
            half = coef.astype(BF16)
            out[:, first * 128 : first * 128 + CHUNK] = half
            part = jnp.dot(half, text, preferred_element_type=F32)
            cot = part if cot is None else cot + part
            sums = terms if sums is None else tuple(a + b for a, b in zip(sums, terms))
    return cot, sums


def own_kernel(scale_ref, bias_ref, y_ref, image_ref, mine_ref, sib_ref, coef_mine, coef_sib, cot_ref, sums_ref):
    cot, sums = pairs(scale_ref, bias_ref, image_ref[...], mine_ref, sib_ref, coef_mine, coef_sib, y_ref[0])
    cot_ref[...] = cot
    for k in range(3):
        sums_ref[k] = sums[k]


def cross_kernel(scale_ref, bias_ref, image_ref, mine_ref, sib_ref, before_ref, coef_mine, coef_sib, cot_ref, sums_ref):
    cot, sums = pairs(scale_ref, bias_ref, image_ref[...], mine_ref, sib_ref, coef_mine, coef_sib)
    cot_ref[...] = cot.astype(BF16)
    lane = lax.broadcasted_iota(jnp.int32, (1, 128), 1)
    row = jnp.zeros((1, 128), F32)
    for k in range(3):
        row = row + jnp.where(lane == k, jnp.sum(sums[k] + before_ref[k]), 0.0)
    sums_ref[...] = row


def text_part(own_ref, cross_ref, image_ref, image_far_ref, block):
    cols = pl.ds(pl.multiple_of(block * 128, 128), 128)
    dims = (((0,), (0,)), ((), ()))
    return lax.dot_general(own_ref[:, cols], image_ref[...], dims, preferred_element_type=F32) + lax.dot_general(
        cross_ref[:, cols], image_far_ref[...], dims, preferred_element_type=F32
    )


def text_sib_kernel(own_ref, cross_ref, image_ref, image_far_ref, sums_ref, out_ref):
    count = (out_ref.shape[0] - EXTRA) // 128
    for k in range(count):
        out_ref[k * 128 : (k + 1) * 128, :] = text_part(own_ref, cross_ref, image_ref, image_far_ref, k).astype(BF16)
    rest = sums_ref[...]
    tail = jnp.zeros((EXTRA, 128), F32)
    row = lax.broadcasted_iota(jnp.int32, (EXTRA, 128), 0)
    for k in range(3):
        term = rest.astype(BF16).astype(F32)
        tail = tail + jnp.where(row == k, term, 0.0)
        rest = rest - term
    out_ref[count * 128 :, 0:128] = tail.astype(BF16)
    out_ref[count * 128 :, 128:] = jnp.zeros((EXTRA, out_ref.shape[1] - 128), BF16)


def text_mine_kernel(y_ref, own_ref, cross_ref, image_ref, image_far_ref, sums_ref, got_ref, spread_ref, *out_refs):
    count = len(out_refs)
    for k in range(count):
        block = lax.rem(y_ref[0] + k, count)
        got = got_ref[pl.ds(pl.multiple_of(block * 128, 128), 128), :]
        total = text_part(own_ref, cross_ref, image_ref, image_far_ref, block) + got.astype(F32)
        out_refs[k][...] = total.astype(out_refs[k].dtype)
    tail = got_ref[count * 128 :, 0:128].astype(F32)
    row = sums_ref[...] + jnp.sum(tail, axis=0, keepdims=True)
    spread_ref[...] = jnp.broadcast_to(row[None], spread_ref.shape)


def pull(embeds, cot, scale):
    floats = embeds.astype(F32)
    cot = jnp.exp(jnp.full((1, floats.shape[1]), scale, F32)) * cot
    inverse = lax.rsqrt(jnp.sum(floats * floats, axis=1, keepdims=True) + EPSILON)
    along = jnp.sum(cot * floats, axis=1, keepdims=True)
    return (inverse * cot - (inverse * inverse * inverse * along) * floats).astype(BF16)


def last_kernel(scale_ref, image_ref, text_ref, image_cot_ref, far_ref, text_cot_ref, *refs):
    *got_refs, totals_ref, image_grad, text_grad, loss_ref, scale_grad, bias_grad = refs
    image_grad[...] = pull(image_ref[...], image_cot_ref[...] + far_ref[...].astype(F32), scale_ref[0])
    cot = text_cot_ref[...]
    for got_ref in got_refs:
        cot = cot + got_ref[...].astype(F32)
    text_grad[...] = pull(text_ref[...], cot, scale_ref[0])
    totals = jnp.sum(totals_ref[...], axis=0)
    lane = lax.broadcasted_iota(jnp.int32, (1, 128), 1)
    batch = 2 * totals_ref.shape[0] * image_ref.shape[0]
    loss, scale, bias = (jnp.sum(jnp.where(lane == k, totals, 0.0)) for k in range(3))
    loss_ref[0] = loss / batch
    scale_grad[0] = scale
    bias_grad[0] = bias


def region(body, inside, *args):
    outs = jax.eval_shape(body, *args)
    return lax.cond(inside, body, lambda *_: jax.tree.map(lambda o: jnp.zeros(o.shape, o.dtype), outs), *args)


def on_device(image_embeds, text_embeds, log_scale, logit_bias):
    rows, width = image_embeds.shape
    y_count = lax.axis_size("y")
    y = jnp.reshape(lax.axis_index("y"), (1,))
    inside = y[0] < y_count
    block, blocks = (rows, width), (y_count, rows, width)
    half = (rows, y_count * rows)
    sum_axes = ("zh", "y", "zl", "x")

    image, text = call(
        norm_kernel,
        [(block, BF16), (blocks, BF16)],
        [HBM] * 2,
        (image_embeds, text_embeds),
        [pltpu.VMEM(block, BF16), pltpu.VMEM(block, BF16), pltpu.SemaphoreType.DMA((2,))],
    )
    image_far = lax.ppermute(image, "zh", SWAP)

    def gather(text):
        mine = lax.all_to_all(text, "y", 0, 0, tiled=True)
        return mine, lax.ppermute(mine, "c", SWAP)

    mine, sib = region(gather, inside, text)
    own_mine, own_sib, image_cot, sums = call(
        own_kernel,
        [(half, BF16), (half, BF16), (block, F32), ((3, 8, 128), F32)],
        [SMEM] * 3 + [VMEM] * 3,
        (log_scale, logit_bias, y, image, mine, sib),
    )
    far_mine, far_sib, far_cot, sums = call(
        cross_kernel,
        [(half, BF16), (half, BF16), (block, BF16), ((1, 128), F32)],
        [SMEM] * 2 + [VMEM] * 4,
        (log_scale, logit_bias, image_far, mine, sib, sums),
    )
    far_got = lax.ppermute(far_cot, "zh", SWAP)

    def text_side(own_mine, own_sib, far_mine, far_sib, image, image_far, y, sums):
        (text_sib,) = call(
            text_sib_kernel,
            [((y_count * rows + EXTRA, width), BF16)],
            [VMEM] * 5,
            (own_sib, far_sib, image, image_far, sums),
        )
        text_got = lax.ppermute(text_sib, "c", SWAP)
        spread, text_kept, *text_send = call(
            text_mine_kernel,
            [((lax.axis_size(sum_axes), 1, 128), F32), (block, F32)] + [(block, BF16)] * (y_count - 1),
            [SMEM] + [VMEM] * 6,
            (y, own_mine, far_mine, image, image_far, sums, text_got),
        )
        got = [
            lax.ppermute(part, "y", [(i, (i + k) % y_count) for i in range(y_count)])
            for k, part in enumerate(text_send, 1)
        ]
        return text_kept, *got, lax.all_to_all(spread, sum_axes, 0, 0, tiled=True)

    text_cots = region(text_side, inside, own_mine, own_sib, far_mine, far_sib, image, image_far, y, sums)
    image_grad, text_grad, loss, scale_grad, bias_grad = call(
        last_kernel,
        [(block, BF16)] * 2 + [((1,), F32)] * 3,
        [SMEM] + [VMEM] * (4 + len(text_cots)),
        (log_scale, image_embeds, text_embeds, image_cot, far_got, *text_cots),
        out_specs=[VMEM] * 2 + [SMEM] * 3,
    )
    return loss, image_grad, text_grad, scale_grad, bias_grad


def solution(mesh):
    fine = Mesh(mesh.devices.reshape(SIZES), AXES)
    return jax.shard_map(
        on_device,
        mesh=fine,
        in_specs=(P(AXES, None), P(AXES, None), P(), P()),
        out_specs=(P(), P(AXES, None), P(AXES, None), P(), P()),
        check_vma=False,
    )
```

```python
import functools

import jax
import jax.numpy as jnp
from jax import lax
from jax.experimental import pallas as pl
from jax.experimental.pallas import tpu as pltpu
from jax.sharding import Mesh, PartitionSpec as P

EPSILON = 1e-06
F32 = jnp.float32
BF16 = jnp.bfloat16
AXES = ("zh", "y", "c", "zl", "x")
SIZES = (2, 4, 2, 8, 4)

VMEM = pl.BlockSpec(memory_space=pltpu.VMEM)
SMEM = pl.BlockSpec(memory_space=pltpu.SMEM)
HBM = pl.BlockSpec(memory_space=pltpu.HBM)
PARAMS = pltpu.CompilerParams(vmem_limit_bytes=16 * 1024 * 1024)
SWAP = ((0, 1), (1, 0))
CHUNK = 256


def call(kernel, outs, in_specs, args, scratch=(), out_specs=None):
    return pl.pallas_call(
        kernel,
        out_shape=[jax.ShapeDtypeStruct(shape, dtype) for shape, dtype in outs],
        in_specs=in_specs,
        out_specs=out_specs or [VMEM] * len(outs),
        scratch_shapes=scratch,
        compiler_params=PARAMS,
    )(*args)


def unit(matrix):
    floats = matrix.astype(F32)
    return (floats * lax.rsqrt(jnp.sum(floats * floats, axis=1, keepdims=True) + EPSILON)).astype(BF16)


def norm_kernel(matrix_ref, *out_refs):
    rows = unit(matrix_ref[...])
    for out_ref in out_refs:
        if len(out_ref.shape) == 2:
            out_ref[...] = rows
        else:
            for k in range(out_ref.shape[0]):
                out_ref[k] = rows


def fold(values):
    rows, cols = values.shape
    total = jnp.sum(values.reshape(rows // 8, 8, cols), axis=0)
    return sum(total[:, k * 128 : (k + 1) * 128] for k in range(cols // 128))


def pair_chunk(image, text, temper, offset, positive):
    products = lax.dot_general(image, text, (((1,), (1,)), ((), ())), preferred_element_type=F32)
    scaled = temper * products
    logits = scaled + offset
    small = jnp.exp(-jnp.abs(logits))
    part = 1.0 / (1.0 + small)
    coef = jnp.where(logits >= 0.0, 1.0, small) * part
    signed = logits
    if positive is not None:
        coef = coef - jnp.where(positive, 1.0, 0.0)
        signed = jnp.where(positive, -logits, logits)
    losses = jnp.maximum(signed, 0.0) + jnp.log1p(small)
    return coef, (fold(losses), fold(coef * scaled), fold(coef))


def pairs(scale_ref, bias_ref, image, mine_ref, sib_ref, coef_mine, coef_sib, y=None):
    per = CHUNK // 128
    temper = jnp.exp(jnp.full((1, CHUNK), scale_ref[0], F32))
    offset = bias_ref[0]
    sums, cot = None, None
    for ref, out in ((mine_ref, coef_mine), (sib_ref, coef_sib)):
        for first in range(0, ref.shape[0], per):
            text = ref[first : first + per].reshape(CHUNK, ref.shape[2])
            positive = None
            if y is not None and ref is mine_ref:
                rows = lax.broadcasted_iota(jnp.int32, (128, CHUNK), 0)
                cols = lax.broadcasted_iota(jnp.int32, (128, CHUNK), 1)
                positive = cols + first * 128 == rows + y * 128
            coef, terms = pair_chunk(image, text, temper, offset, positive)
            half = coef.astype(BF16)
            out[:, first * 128 : first * 128 + CHUNK] = half
            part = jnp.dot(half, text, preferred_element_type=F32)
            cot = part if cot is None else cot + part
            sums = terms if sums is None else tuple(a + b for a, b in zip(sums, terms))
    return cot, sums


def own_kernel(
    scale_ref, bias_ref, y_ref, image_ref, mine_ref, sib_ref, coef_mine, coef_sib, cot_ref, sums_ref, mine_out, sib_out
):
    mine_out[...] = mine_ref[...]
    sib_out[...] = sib_ref[...]
    cot, sums = pairs(scale_ref, bias_ref, image_ref[...], mine_ref, sib_ref, coef_mine, coef_sib, y_ref[0])
    cot_ref[...] = cot
    for k in range(3):
        sums_ref[k] = sums[k]


def cross_kernel(scale_ref, bias_ref, image_ref, mine_ref, sib_ref, before_ref, coef_mine, coef_sib, cot_ref, sums_ref):
    cot, sums = pairs(scale_ref, bias_ref, image_ref[...], mine_ref, sib_ref, coef_mine, coef_sib)
    cot_ref[...] = cot.astype(BF16)
    for k in range(3):
        total = sums[k] + before_ref[k]
        for peer in range(sums_ref.shape[0]):
            sums_ref[peer, k * 8 : (k + 1) * 8] = total


def text_part(own_ref, cross_ref, image_ref, image_far_ref, block):
    cols = pl.ds(pl.multiple_of(block * 128, 128), 128)
    dims = (((0,), (0,)), ((), ()))
    return lax.dot_general(own_ref[:, cols], image_ref[...], dims, preferred_element_type=F32) + lax.dot_general(
        cross_ref[:, cols], image_far_ref[...], dims, preferred_element_type=F32
    )


def text_sib_kernel(own_ref, cross_ref, image_ref, image_far_ref, out_ref):
    for k in range(out_ref.shape[0]):
        out_ref[k] = text_part(own_ref, cross_ref, image_ref, image_far_ref, k).astype(BF16)


def text_mine_kernel(y_ref, own_ref, cross_ref, image_ref, image_far_ref, near_ref, got_ref, spread_ref, *out_refs):
    count = len(out_refs)
    for k in range(count):
        block = lax.rem(y_ref[0] + k, count)
        total = text_part(own_ref, cross_ref, image_ref, image_far_ref, block) + got_ref[block].astype(F32)
        out_refs[k][...] = total.astype(out_refs[k].dtype)
    near = jnp.sum(near_ref[...], axis=0)
    lane = lax.broadcasted_iota(jnp.int32, (1, 128), 1)
    row = jnp.zeros((1, 128), F32)
    for k in range(3):
        row = row + jnp.where(lane == k, jnp.sum(near[k * 8 : (k + 1) * 8]), 0.0)
    spread_ref[...] = jnp.broadcast_to(row[None], spread_ref.shape)


def pull(embeds, cot, scale):
    floats = embeds.astype(F32)
    cot = jnp.exp(jnp.full((1, floats.shape[1]), scale, F32)) * cot
    inverse = lax.rsqrt(jnp.sum(floats * floats, axis=1, keepdims=True) + EPSILON)
    along = jnp.sum(cot * floats, axis=1, keepdims=True)
    return (inverse * cot - (inverse * inverse * inverse * along) * floats).astype(BF16)


def last_kernel(batch, scale_ref, image_ref, text_ref, image_cot_ref, far_ref, text_cot_ref, *refs):
    *got_refs, totals_ref, image_grad, text_grad, loss_ref, scale_grad, bias_grad = refs
    image_grad[...] = pull(image_ref[...], image_cot_ref[...] + far_ref[...].astype(F32), scale_ref[0])
    cot = text_cot_ref[...]
    for got_ref in got_refs:
        cot = cot + got_ref[...].astype(F32)
    text_grad[...] = pull(text_ref[...], cot, scale_ref[0])
    totals = jnp.sum(totals_ref[...], axis=0)
    lane = lax.broadcasted_iota(jnp.int32, (1, 128), 1)
    loss, scale, bias = (jnp.sum(jnp.where(lane == k, totals, 0.0)) for k in range(3))
    loss_ref[0] = loss / batch
    scale_grad[0] = scale
    bias_grad[0] = bias


def region(body, inside, *args):
    outs = jax.eval_shape(body, *args)
    return lax.cond(inside, body, lambda *_: jax.tree.map(lambda o: jnp.zeros(o.shape, o.dtype), outs), *args)


def on_device(image_embeds, text_embeds, log_scale, logit_bias):
    rows, width = image_embeds.shape
    y_count = lax.axis_size("y")
    y = jnp.reshape(lax.axis_index("y"), (1,))
    inside = y[0] < y_count
    block, blocks = (rows, width), (y_count, rows, width)
    half = (rows, y_count * rows)

    (image,) = call(norm_kernel, [(block, BF16)], [VMEM], (image_embeds,))
    image_far = lax.ppermute(image, "zh", SWAP)

    def gather(text_embeds):
        (text,) = call(norm_kernel, [(blocks, BF16)], [VMEM], (text_embeds,))
        mine = lax.all_to_all(text, "y", 0, 0, tiled=True)
        return mine, lax.ppermute(mine, "c", SWAP)

    mine, sib = region(gather, inside, text_embeds)
    own_mine, own_sib, image_cot, sums, mine, sib = call(
        own_kernel,
        [(half, BF16), (half, BF16), (block, F32), ((3, 8, 128), F32), (blocks, BF16), (blocks, BF16)],
        [SMEM] * 3 + [VMEM] * 3,
        (log_scale, logit_bias, y, image, mine, sib),
    )
    far_mine, far_sib, far_cot, sums = call(
        cross_kernel,
        [(half, BF16), (half, BF16), (block, BF16), ((lax.axis_size(("y", "c", "x")), 24, 128), F32)],
        [SMEM] * 2 + [VMEM] * 4,
        (log_scale, logit_bias, image_far, mine, sib, sums),
    )
    far_got = lax.ppermute(far_cot, "zh", SWAP)

    (text_sib,) = call(text_sib_kernel, [(blocks, BF16)], [VMEM] * 4, (own_sib, far_sib, image, image_far))
    text_got = lax.ppermute(text_sib, "c", SWAP)
    near = lax.all_to_all(sums, ("y", "c", "x"), 0, 0, tiled=True)

    def text_side(own_mine, far_mine, image, image_far, y, near, text_got):
        z_axes = ("zh", "zl")
        spread, text_kept, *text_send = call(
            text_mine_kernel,
            [((lax.axis_size(z_axes), 1, 128), F32), (block, F32)] + [(block, BF16)] * (y_count - 1),
            [SMEM] + [VMEM] * 6,
            (y, own_mine, far_mine, image, image_far, near, text_got),
        )
        got = [
            lax.ppermute(part, "y", [(i, (i + k) % y_count) for i in range(y_count)])
            for k, part in enumerate(text_send, 1)
        ]
        totals = region(lambda v: lax.all_to_all(v, z_axes, 0, 0, tiled=True), y[0] < y_count, spread)
        return text_kept, *got, totals

    text_cots = region(text_side, inside, own_mine, far_mine, image, image_far, y, near, text_got)
    image_grad, text_grad, loss, scale_grad, bias_grad = call(
        functools.partial(last_kernel, rows * lax.axis_size(AXES)),
        [(block, BF16)] * 2 + [((1,), F32)] * 3,
        [SMEM] + [VMEM] * (4 + len(text_cots)),
        (log_scale, image_embeds, text_embeds, image_cot, far_got, *text_cots),
        out_specs=[VMEM] * 2 + [SMEM] * 3,
    )
    return loss, image_grad, text_grad, scale_grad, bias_grad


def solution(mesh):
    fine = Mesh(mesh.devices.reshape(SIZES), AXES)
    return jax.shard_map(
        on_device,
        mesh=fine,
        in_specs=(P(AXES, None), P(AXES, None), P(), P()),
        out_specs=(P(), P(AXES, None), P(AXES, None), P(), P()),
        check_vma=False,
    )
```

```python
import functools

import jax
import jax.numpy as jnp
from jax import lax
from jax.experimental import pallas as pl
from jax.experimental.pallas import tpu as pltpu
from jax.sharding import Mesh, PartitionSpec as P

EPSILON = 1e-06
F32 = jnp.float32
BF16 = jnp.bfloat16
AXES = ("zh", "y", "c", "zl", "x")
SIZES = (2, 4, 2, 8, 4)

VMEM = pl.BlockSpec(memory_space=pltpu.VMEM)
SMEM = pl.BlockSpec(memory_space=pltpu.SMEM)
HBM = pl.BlockSpec(memory_space=pltpu.HBM)
PARAMS = pltpu.CompilerParams(vmem_limit_bytes=16 * 1024 * 1024)
SWAP = ((0, 1), (1, 0))
CHUNK = 256


def call(kernel, outs, in_specs, args, scratch=(), out_specs=None):
    return pl.pallas_call(
        kernel,
        out_shape=[jax.ShapeDtypeStruct(shape, dtype) for shape, dtype in outs],
        in_specs=in_specs,
        out_specs=out_specs or [VMEM] * len(outs),
        scratch_shapes=scratch,
        compiler_params=PARAMS,
    )(*args)


def unit(matrix):
    floats = matrix.astype(F32)
    return (floats * lax.rsqrt(jnp.sum(floats * floats, axis=1, keepdims=True) + EPSILON)).astype(BF16)


def norm_kernel(matrix_ref, *out_refs):
    rows = unit(matrix_ref[...])
    for out_ref in out_refs:
        if len(out_ref.shape) == 2:
            out_ref[...] = rows
        else:
            for k in range(out_ref.shape[0]):
                out_ref[k] = rows


def fold(values):
    rows, cols = values.shape
    total = jnp.sum(values.reshape(rows // 8, 8, cols), axis=0)
    return sum(total[:, k * 128 : (k + 1) * 128] for k in range(cols // 128))


def pair_chunk(image, text, temper, offset, positive):
    products = lax.dot_general(image, text, (((1,), (1,)), ((), ())), preferred_element_type=F32)
    scaled = temper * products
    logits = scaled + offset
    small = jnp.exp(-jnp.abs(logits))
    part = 1.0 / (1.0 + small)
    coef = jnp.where(logits >= 0.0, 1.0, small) * part
    signed = logits
    if positive is not None:
        coef = coef - jnp.where(positive, 1.0, 0.0)
        signed = jnp.where(positive, -logits, logits)
    losses = jnp.maximum(signed, 0.0) + jnp.log1p(small)
    return coef, (fold(losses), fold(coef * scaled), fold(coef))


def pairs(scale_ref, bias_ref, image, mine_ref, sib_ref, coef_mine, coef_sib, y=None):
    per = CHUNK // 128
    temper = jnp.exp(jnp.full((1, CHUNK), scale_ref[0], F32))
    offset = bias_ref[0]
    sums, cot = None, None
    for ref, out in ((mine_ref, coef_mine), (sib_ref, coef_sib)):
        for first in range(0, ref.shape[0], per):
            text = ref[first : first + per].reshape(CHUNK, ref.shape[2])
            positive = None
            if y is not None and ref is mine_ref:
                rows = lax.broadcasted_iota(jnp.int32, (128, CHUNK), 0)
                cols = lax.broadcasted_iota(jnp.int32, (128, CHUNK), 1)
                positive = cols + first * 128 == rows + y * 128
            coef, terms = pair_chunk(image, text, temper, offset, positive)
            half = coef.astype(BF16)
            out[:, first * 128 : first * 128 + CHUNK] = half
            part = jnp.dot(half, text, preferred_element_type=F32)
            cot = part if cot is None else cot + part
            sums = terms if sums is None else tuple(a + b for a, b in zip(sums, terms))
    return cot, sums


def own_kernel(
    scale_ref,
    bias_ref,
    y_ref,
    image_ref,
    mine_ref,
    sib_ref,
    coef_mine,
    coef_sib,
    cot_ref,
    sums_ref,
    mine_out,
    sib_out,
    image_out,
):
    mine_out[...] = mine_ref[...]
    sib_out[...] = sib_ref[...]
    image = unit(image_ref[...])
    image_out[...] = image
    cot, sums = pairs(scale_ref, bias_ref, image, mine_ref, sib_ref, coef_mine, coef_sib, y_ref[0])
    cot_ref[...] = cot
    for k in range(3):
        sums_ref[k * 8 : (k + 1) * 8] = sums[k]


def cross_kernel(
    scale_ref,
    bias_ref,
    image_ref,
    mine_ref,
    sib_ref,
    before_ref,
    coef_mine,
    coef_sib,
    cot_ref,
    sums_ref,
    image_out,
):
    image = unit(image_ref[...])
    image_out[...] = image
    cot, sums = pairs(scale_ref, bias_ref, image, mine_ref, sib_ref, coef_mine, coef_sib)
    cot_ref[...] = cot.astype(BF16)
    for k in range(3):
        rows = slice(k * 8, (k + 1) * 8)
        sums_ref[rows] = sums[k] + before_ref[rows]


def text_part(own_ref, cross_ref, image_ref, image_far_ref, block):
    cols = pl.ds(pl.multiple_of(block * 128, 128), 128)
    dims = (((0,), (0,)), ((), ()))
    return lax.dot_general(own_ref[:, cols], image_ref[...], dims, preferred_element_type=F32) + lax.dot_general(
        cross_ref[:, cols], image_far_ref[...], dims, preferred_element_type=F32
    )


def text_sib_kernel(own_ref, cross_ref, image_ref, image_far_ref, out_ref):
    for k in range(out_ref.shape[0]):
        out_ref[k] = text_part(own_ref, cross_ref, image_ref, image_far_ref, k).astype(BF16)


def text_mine_kernel(y_ref, own_ref, cross_ref, image_ref, image_far_ref, got_ref, sums_ref, spread_ref, *out_refs):
    spread_ref[...] = jnp.broadcast_to(sums_ref[...][None], spread_ref.shape)
    count = len(out_refs)
    for k in range(count):
        block = lax.rem(y_ref[0] + k, count)
        total = text_part(own_ref, cross_ref, image_ref, image_far_ref, block) + got_ref[block].astype(F32)
        out_refs[k][...] = total.astype(out_refs[k].dtype)


def sum_kernel(near_ref, spread_ref):
    near = jnp.sum(near_ref[...], axis=0)
    lane = lax.broadcasted_iota(jnp.int32, (1, 128), 1)
    row = jnp.zeros((1, 128), F32)
    for k in range(3):
        row = row + jnp.where(lane == k, jnp.sum(near[k * 8 : (k + 1) * 8]), 0.0)
    spread_ref[...] = jnp.broadcast_to(row[None], spread_ref.shape)


def pull(embeds, cot, scale):
    floats = embeds.astype(F32)
    cot = jnp.exp(jnp.full((1, floats.shape[1]), scale, F32)) * cot
    inverse = lax.rsqrt(jnp.sum(floats * floats, axis=1, keepdims=True) + EPSILON)
    along = jnp.sum(cot * floats, axis=1, keepdims=True)
    return (inverse * cot - (inverse * inverse * inverse * along) * floats).astype(BF16)


def grad_kernel(scale_ref, embeds_ref, cot_ref, *refs):
    cot = cot_ref[...]
    for got_ref in refs[:-1]:
        cot = cot + got_ref[...].astype(F32)
    refs[-1][...] = pull(embeds_ref[...], cot, scale_ref[0])


def last_kernel(batch, scale_ref, embeds_ref, cot_ref, got_ref, totals_ref, grad_ref, loss_ref, scale_grad, bias_grad):
    grad_kernel(scale_ref, embeds_ref, cot_ref, got_ref, grad_ref)
    totals = jnp.sum(totals_ref[...], axis=0)
    lane = lax.broadcasted_iota(jnp.int32, (1, 128), 1)
    loss, scale, bias = (jnp.sum(jnp.where(lane == k, totals, 0.0)) for k in range(3))
    loss_ref[0] = loss / batch
    scale_grad[0] = scale
    bias_grad[0] = bias


def region(body, inside, *args):
    outs = jax.eval_shape(body, *args)
    return lax.cond(inside, body, lambda *_: jax.tree.map(lambda o: jnp.zeros(o.shape, o.dtype), outs), *args)


def on_device(image_embeds, text_embeds, log_scale, logit_bias):
    rows, width = image_embeds.shape
    y_count = lax.axis_size("y")
    y = jnp.reshape(lax.axis_index("y"), (1,))
    inside = y[0] < y_count
    block, blocks = (rows, width), (y_count, rows, width)
    half = (rows, y_count * rows)

    image_far = lax.ppermute(image_embeds, "zh", SWAP)
    (text,) = call(norm_kernel, [(blocks, BF16)], [VMEM], (text_embeds,))

    def gather(text):
        mine = lax.all_to_all(text, "y", 0, 0, tiled=True)
        return mine, lax.ppermute(mine, "c", SWAP)

    mine, sib = region(gather, inside, text)
    own_mine, own_sib, image_cot, sums, mine, sib, image = call(
        own_kernel,
        [(half, BF16), (half, BF16), (block, F32), ((24, 128), F32), (blocks, BF16), (blocks, BF16), (block, BF16)],
        [SMEM] * 3 + [VMEM] * 3,
        (log_scale, logit_bias, y, image_embeds, mine, sib),
    )
    far_mine, far_sib, far_cot, sums, image_far = call(
        cross_kernel,
        [(half, BF16), (half, BF16), (block, BF16), ((24, 128), F32), (block, BF16)],
        [SMEM] * 2 + [VMEM] * 4,
        (log_scale, logit_bias, image_far, mine, sib, sums),
    )
    far_got = lax.ppermute(far_cot, "zh", SWAP)

    (text_sib,) = call(text_sib_kernel, [(blocks, BF16)], [VMEM] * 4, (own_sib, far_sib, image, image_far))
    text_got = lax.ppermute(text_sib, "c", SWAP)

    def text_side(own_mine, far_mine, image, image_far, text_got, y, sums, text_embeds, log_scale):
        near_axes = ("y", "c", "x")
        spread, text_kept, *text_send = call(
            text_mine_kernel,
            [((lax.axis_size(near_axes), 24, 128), F32), (block, F32)] + [(block, BF16)] * (y_count - 1),
            [SMEM] + [VMEM] * 6,
            (y, own_mine, far_mine, image, image_far, text_got, sums),
        )
        near = lax.all_to_all(spread, near_axes, 0, 0, tiled=True)
        got = [
            lax.ppermute(part, "y", [(i, (i + k) % y_count) for i in range(y_count)])
            for k, part in enumerate(text_send, 1)
        ]
        z_axes = ("zh", "zl")
        (spread,) = call(sum_kernel, [((lax.axis_size(z_axes), 1, 128), F32)], [VMEM], (near,))
        totals = lax.all_to_all(spread, z_axes, 0, 0, tiled=True)
        (text_grad,) = call(
            grad_kernel,
            [(block, BF16)],
            [SMEM] + [VMEM] * (2 + len(got)),
            (log_scale, text_embeds, text_kept, *got),
        )
        return text_grad, totals

    text_grad, totals = region(
        text_side,
        inside,
        own_mine,
        far_mine,
        image,
        image_far,
        text_got,
        y,
        sums,
        text_embeds,
        log_scale,
    )
    image_grad, loss, scale_grad, bias_grad = call(
        functools.partial(last_kernel, rows * lax.axis_size(AXES)),
        [(block, BF16)] + [((1,), F32)] * 3,
        [SMEM] + [VMEM] * 4,
        (log_scale, image_embeds, image_cot, far_got, totals),
        out_specs=[VMEM] + [SMEM] * 3,
    )
    return loss, image_grad, text_grad, scale_grad, bias_grad


def solution(mesh):
    fine = Mesh(mesh.devices.reshape(SIZES), AXES)
    return jax.shard_map(
        on_device,
        mesh=fine,
        in_specs=(P(AXES, None), P(AXES, None), P(), P()),
        out_specs=(P(), P(AXES, None), P(AXES, None), P(), P()),
        check_vma=False,
    )
```

```python
import functools

import jax
import jax.numpy as jnp
from jax import lax
from jax.experimental import pallas as pl
from jax.experimental.pallas import tpu as pltpu
from jax.sharding import Mesh, PartitionSpec as P

EPSILON = 1e-06
F32 = jnp.float32
BF16 = jnp.bfloat16
AXES = ("zh", "y", "c", "zl", "x")
SIZES = (2, 4, 2, 8, 4)

VMEM = pl.BlockSpec(memory_space=pltpu.VMEM)
SMEM = pl.BlockSpec(memory_space=pltpu.SMEM)
HBM = pl.BlockSpec(memory_space=pltpu.HBM)
PARAMS = pltpu.CompilerParams(vmem_limit_bytes=16 * 1024 * 1024)
SWAP = ((0, 1), (1, 0))
CHUNK = 256


def call(kernel, outs, in_specs, args, scratch=(), out_specs=None):
    return pl.pallas_call(
        kernel,
        out_shape=[jax.ShapeDtypeStruct(shape, dtype) for shape, dtype in outs],
        in_specs=in_specs,
        out_specs=out_specs or [VMEM] * len(outs),
        scratch_shapes=scratch,
        compiler_params=PARAMS,
    )(*args)


def unit(matrix):
    floats = matrix.astype(F32)
    return (floats * lax.rsqrt(jnp.sum(floats * floats, axis=1, keepdims=True) + EPSILON)).astype(BF16)


def first_kernel(scale_ref, bias_ref, text_ref, text_out, scalars_ref, scale, bias, sems):
    copies = [
        pltpu.make_async_copy(scale_ref, scale, sems.at[0]),
        pltpu.make_async_copy(bias_ref, bias, sems.at[1]),
    ]
    for copy in copies:
        copy.start()
    rows = unit(text_ref[...])
    for k in range(text_out.shape[0]):
        text_out[k] = rows
    for copy in copies:
        copy.wait()
    row = lax.broadcasted_iota(jnp.int32, scalars_ref.shape, 0)
    temper = jnp.exp(jnp.full(scalars_ref.shape, scale[0], F32))
    scalars_ref[...] = jnp.where(row == 0, temper, bias[0])


def fold(values):
    rows, cols = values.shape
    total = jnp.sum(values.reshape(rows // 8, 8, cols), axis=0)
    return sum(total[:, k * 128 : (k + 1) * 128] for k in range(cols // 128))


def pair_chunk(image, text, temper, offset, positive):
    products = lax.dot_general(image, text, (((1,), (1,)), ((), ())), preferred_element_type=F32)
    scaled = temper * products
    logits = scaled + offset
    small = jnp.exp(-jnp.abs(logits))
    part = 1.0 / (1.0 + small)
    coef = jnp.where(logits >= 0.0, 1.0, small) * part
    signed = logits
    if positive is not None:
        coef = coef - jnp.where(positive, 1.0, 0.0)
        signed = jnp.where(positive, -logits, logits)
    losses = jnp.maximum(signed, 0.0) + jnp.log1p(small)
    return coef, (fold(losses), fold(coef * scaled), fold(coef))


def pairs(scalars_ref, image, text_ref, coef_ref, y=None):
    per = CHUNK // 128
    temper = scalars_ref[0:1, 0:1]
    offset = scalars_ref[1:2, 0:1]
    sums, cot = None, None
    for first in range(0, text_ref.shape[0], per):
        text = text_ref[first : first + per].reshape(CHUNK, text_ref.shape[2])
        positive = None
        if y is not None:
            rows = lax.broadcasted_iota(jnp.int32, (128, CHUNK), 0)
            cols = lax.broadcasted_iota(jnp.int32, (128, CHUNK), 1)
            positive = cols + first * 128 == rows + y * 128
        coef, terms = pair_chunk(image, text, temper, offset, positive)
        half = coef.astype(BF16)
        coef_ref[:, first * 128 : first * 128 + CHUNK] = half
        part = jnp.dot(half, text, preferred_element_type=F32)
        cot = part if cot is None else cot + part
        sums = terms if sums is None else tuple(a + b for a, b in zip(sums, terms))
    return cot, jnp.concatenate(sums, axis=0)


def own_mine_kernel(scalars_ref, y_ref, image_ref, text_ref, coef_ref, cot_ref, sums_ref, image_out):
    image = unit(image_ref[...])
    image_out[...] = image
    cot_ref[...], sums_ref[...] = pairs(scalars_ref, image, text_ref, coef_ref, y_ref[0])


def own_sib_kernel(
    scalars_ref,
    image_ref,
    mine_ref,
    sib_ref,
    before_cot,
    before_sums,
    coef_ref,
    cot_ref,
    sums_ref,
    mine_out,
    sib_out,
):
    mine_out[...] = mine_ref[...]
    sib_out[...] = sib_ref[...]
    cot, sums = pairs(scalars_ref, image_ref[...], sib_ref, coef_ref)
    cot_ref[...] = before_cot[...] + cot
    sums_ref[...] = before_sums[...] + sums


def cross_kernel(
    scalars_ref,
    image_ref,
    image_far_ref,
    own_sib,
    mine_ref,
    sib_ref,
    before_sums,
    coef_mine,
    cot_ref,
    sums_ref,
    image_out,
    text_sib,
    coef_sib,
):
    image = unit(image_far_ref[...])
    image_out[...] = image
    cot, sums = pairs(scalars_ref, image, sib_ref, coef_sib)
    for k in range(text_sib.shape[0]):
        text_sib[k] = text_part(own_sib, coef_sib, image_ref, image_out, k).astype(BF16)
    more_cot, more_sums = pairs(scalars_ref, image, mine_ref, coef_mine)
    cot_ref[...] = (cot + more_cot).astype(BF16)
    sums_ref[...] = before_sums[...] + sums + more_sums


def text_part(own_ref, cross_ref, image_ref, image_far_ref, block):
    cols = pl.ds(pl.multiple_of(block * 128, 128), 128)
    dims = (((0,), (0,)), ((), ()))
    return lax.dot_general(own_ref[:, cols], image_ref[...], dims, preferred_element_type=F32) + lax.dot_general(
        cross_ref[:, cols], image_far_ref[...], dims, preferred_element_type=F32
    )


def text_mine_kernel(y_ref, own_ref, cross_ref, image_ref, image_far_ref, got_ref, sums_ref, spread_ref, *out_refs):
    spread_ref[...] = jnp.broadcast_to(sums_ref[...][None], spread_ref.shape)
    count = len(out_refs)
    for k in range(count):
        block = lax.rem(y_ref[0] + k, count)
        total = text_part(own_ref, cross_ref, image_ref, image_far_ref, block) + got_ref[block].astype(F32)
        out_refs[k][...] = total.astype(out_refs[k].dtype)


def sum_kernel(near_ref, spread_ref):
    near = jnp.sum(near_ref[...], axis=0)
    lane = lax.broadcasted_iota(jnp.int32, (1, 128), 1)
    row = jnp.zeros((1, 128), F32)
    for k in range(3):
        row = row + jnp.where(lane == k, jnp.sum(near[k * 8 : (k + 1) * 8]), 0.0)
    spread_ref[...] = jnp.broadcast_to(row[None], spread_ref.shape)


def pull(embeds, cot, temper):
    floats = embeds.astype(F32)
    cot = temper * cot
    inverse = lax.rsqrt(jnp.sum(floats * floats, axis=1, keepdims=True) + EPSILON)
    along = jnp.sum(cot * floats, axis=1, keepdims=True)
    return (inverse * cot - (inverse * inverse * inverse * along) * floats).astype(BF16)


def grad_kernel(scalars_ref, embeds_ref, cot_ref, *refs):
    cot = cot_ref[...]
    for got_ref in refs[:-1]:
        cot = cot + got_ref[...].astype(F32)
    refs[-1][...] = pull(embeds_ref[...], cot, scalars_ref[0:1, 0:1])


def last_kernel(batch, scalars_ref, embeds_ref, cot_ref, got_ref, totals_ref, grad_ref, loss_ref, scale_grad, bias_grad):
    grad_kernel(scalars_ref, embeds_ref, cot_ref, got_ref, grad_ref)
    totals = jnp.sum(totals_ref[...], axis=0)
    lane = lax.broadcasted_iota(jnp.int32, (1, 128), 1)
    loss, scale, bias = (jnp.sum(jnp.where(lane == k, totals, 0.0)) for k in range(3))
    loss_ref[0] = loss / batch
    scale_grad[0] = scale
    bias_grad[0] = bias


def region(body, inside, *args):
    outs = jax.eval_shape(body, *args)
    return lax.cond(inside, body, lambda *_: jax.tree.map(lambda o: jnp.zeros(o.shape, o.dtype), outs), *args)


def on_device(image_embeds, text_embeds, log_scale, logit_bias):
    rows, width = image_embeds.shape
    y_count = lax.axis_size("y")
    y = jnp.reshape(lax.axis_index("y"), (1,))
    inside = y[0] < y_count
    block, blocks = (rows, width), (y_count, rows, width)
    half = (rows, y_count * rows)

    image_far = lax.ppermute(image_embeds, "zh", SWAP)
    text, scalars = call(
        first_kernel,
        [(blocks, BF16), ((8, 128), F32)],
        [HBM, HBM, VMEM],
        (log_scale, logit_bias, text_embeds),
        [pltpu.SMEM((1,), F32), pltpu.SMEM((1,), F32), pltpu.SemaphoreType.DMA((2,))],
    )

    def own_pairs(text, image_embeds, scalars, y):
        mine = lax.all_to_all(text, "y", 0, 0, tiled=True)
        sib = lax.ppermute(mine, "c", SWAP)
        coef, cot, sums, image = call(
            own_mine_kernel,
            [(half, BF16), (block, F32), ((24, 128), F32), (block, BF16)],
            [VMEM, SMEM, VMEM, VMEM],
            (scalars, y, image_embeds, mine),
        )
        return mine, sib, coef, cot, sums, image

    mine, sib, own_mine, image_cot, sums, image = region(
        own_pairs, inside, text, image_embeds, scalars, y
    )
    own_sib, image_cot, sums, mine, sib = call(
        own_sib_kernel,
        [(half, BF16), (block, F32), ((24, 128), F32), (blocks, BF16), (blocks, BF16)],
        [VMEM] * 6,
        (scalars, image, mine, sib, image_cot, sums),
    )
    far_mine, far_cot, sums, image_far, text_sib = call(
        cross_kernel,
        [(half, BF16), (block, BF16), ((24, 128), F32), (block, BF16), (blocks, BF16)],
        [VMEM] * 7,
        (scalars, image, image_far, own_sib, mine, sib, sums),
        [pltpu.VMEM(half, BF16)],
    )
    far_got = lax.ppermute(far_cot, "zh", SWAP)

    text_got = lax.ppermute(text_sib, "c", SWAP)

    def text_side(own_mine, far_mine, image, image_far, text_got, y, sums, text_embeds, scalars):
        near_axes = ("y", "c", "x")
        spread, text_kept, *text_send = call(
            text_mine_kernel,
            [((lax.axis_size(near_axes), 24, 128), F32), (block, F32)] + [(block, BF16)] * (y_count - 1),
            [SMEM] + [VMEM] * 6,
            (y, own_mine, far_mine, image, image_far, text_got, sums),
        )
        near = lax.all_to_all(spread, near_axes, 0, 0, tiled=True)
        got = [
            lax.ppermute(part, "y", [(i, (i + k) % y_count) for i in range(y_count)])
            for k, part in enumerate(text_send, 1)
        ]
        z_axes = ("zh", "zl")
        (spread,) = call(sum_kernel, [((lax.axis_size(z_axes), 1, 128), F32)], [VMEM], (near,))
        totals = lax.all_to_all(spread, z_axes, 0, 0, tiled=True)
        (text_grad,) = call(
            grad_kernel,
            [(block, BF16)],
            [VMEM] * (3 + len(got)),
            (scalars, text_embeds, text_kept, *got),
        )
        return text_grad, totals

    text_grad, totals = region(
        text_side,
        inside,
        own_mine,
        far_mine,
        image,
        image_far,
        text_got,
        y,
        sums,
        text_embeds,
        scalars,
    )
    image_grad, loss, scale_grad, bias_grad = call(
        functools.partial(last_kernel, rows * lax.axis_size(AXES)),
        [(block, BF16)] + [((1,), F32)] * 3,
        [VMEM] * 5,
        (scalars, image_embeds, image_cot, far_got, totals),
        out_specs=[VMEM] + [SMEM] * 3,
    )
    return loss, image_grad, text_grad, scale_grad, bias_grad


def solution(mesh):
    fine = Mesh(mesh.devices.reshape(SIZES), AXES)
    return jax.shard_map(
        on_device,
        mesh=fine,
        in_specs=(P(AXES, None), P(AXES, None), P(), P()),
        out_specs=(P(), P(AXES, None), P(AXES, None), P(), P()),
        check_vma=False,
    )
```

```python
import functools

import jax
import jax.numpy as jnp
from jax import lax
from jax.experimental import pallas as pl
from jax.experimental.pallas import tpu as pltpu
from jax.sharding import Mesh, PartitionSpec as P

EPSILON = 1e-06
F32 = jnp.float32
BF16 = jnp.bfloat16
AXES = ("zh", "y", "c", "zl", "x")
SIZES = (2, 4, 2, 8, 4)

VMEM = pl.BlockSpec(memory_space=pltpu.VMEM)
SMEM = pl.BlockSpec(memory_space=pltpu.SMEM)
PARAMS = pltpu.CompilerParams(vmem_limit_bytes=16 * 1024 * 1024)
SWAP = ((0, 1), (1, 0))
CHUNK = 256
PART = 16


def call(kernel, outs, in_specs, args, scratch=(), out_specs=None):
    return pl.pallas_call(
        kernel,
        out_shape=[jax.ShapeDtypeStruct(shape, dtype) for shape, dtype in outs],
        in_specs=in_specs,
        out_specs=out_specs or [VMEM] * len(outs),
        scratch_shapes=scratch,
        compiler_params=PARAMS,
    )(*args)


def unit(matrix):
    floats = matrix.astype(F32)
    return (floats * lax.rsqrt(jnp.sum(floats * floats, axis=1, keepdims=True) + EPSILON)).astype(BF16)


def norm_kernel(matrix_ref, out_ref):
    rows = unit(matrix_ref[...])
    for k in range(out_ref.shape[0]):
        out_ref[k] = rows


def scalars_kernel(scale_ref, bias_ref, scalars_ref):
    row = lax.broadcasted_iota(jnp.int32, scalars_ref.shape, 0)
    temper = jnp.exp(jnp.full(scalars_ref.shape, scale_ref[0], F32))
    scalars_ref[...] = jnp.where(row == 0, temper, bias_ref[0])


def lanes(values):
    return sum(values[:, k * 128 : (k + 1) * 128] for k in range(values.shape[1] // 128))


def fold(values):
    rows, cols = values.shape
    return lanes(jnp.sum(values.reshape(rows // PART, PART, cols), axis=0))


def fold_logs(values):
    rows, cols = values.shape
    parts = values.reshape(rows // PART, PART, cols)
    while parts.shape[0] > 1:
        middle = parts.shape[0] // 2
        parts = parts[:middle] * parts[middle:]
    return lanes(jnp.log(parts[0]))


def pair_chunk(image, text, temper, offset, positive):
    products = lax.dot_general(image, text, (((1,), (1,)), ((), ())), preferred_element_type=F32)
    scaled = temper * products
    logits = scaled + offset
    small = jnp.exp(-jnp.abs(logits))
    part = 1.0 / (1.0 + small)
    coef = jnp.where(logits >= 0.0, 1.0, small) * part
    signed = logits
    if positive is not None:
        coef = coef - jnp.where(positive, 1.0, 0.0)
        signed = jnp.where(positive, -logits, logits)
    loss = fold(jnp.maximum(signed, 0.0)) + fold_logs(1.0 + small)
    return coef, (loss, fold(coef * scaled), fold(coef))


def pairs(scalars_ref, image, text_ref, coef_ref, y=None, pull_back=True):
    per = CHUNK // 128
    temper = scalars_ref[0:1, 0:1]
    offset = scalars_ref[1:2, 0:1]
    sums, cot = None, None
    for first in range(0, text_ref.shape[0], per):
        text = text_ref[first : first + per].reshape(CHUNK, text_ref.shape[2])
        positive = None
        if y is not None:
            rows = lax.broadcasted_iota(jnp.int32, (128, CHUNK), 0)
            cols = lax.broadcasted_iota(jnp.int32, (128, CHUNK), 1)
            positive = cols + first * 128 == rows + y * 128
        coef, terms = pair_chunk(image, text, temper, offset, positive)
        half = coef.astype(BF16)
        coef_ref[:, first * 128 : first * 128 + CHUNK] = half
        if pull_back:
            part = jnp.dot(half, text, preferred_element_type=F32)
            cot = part if cot is None else cot + part
        sums = terms if sums is None else tuple(a + b for a, b in zip(sums, terms))
    return cot, jnp.concatenate(sums, axis=0)


def own_mine_kernel(
    scalars_ref, y_ref, image_ref, text_ref, coef_ref, sums_ref, image_out, text_out
):
    text_out[...] = text_ref[...]
    image = unit(image_ref[...])
    image_out[...] = image
    _, sums_ref[...] = pairs(scalars_ref, image, text_ref, coef_ref, y_ref[0], False)


def own_sib_kernel(
    scalars_ref,
    image_ref,
    sib_ref,
    mine_ref,
    coef_mine,
    before_sums,
    coef_ref,
    cot_ref,
    sums_ref,
    sib_out,
    scalars_out,
):
    scalars_out[...] = scalars_ref[...]
    sib_out[...] = sib_ref[...]
    cot, sums = pairs(scalars_ref, image_ref[...], sib_ref, coef_ref)
    per = CHUNK // 128
    for first in range(0, mine_ref.shape[0], per):
        text = mine_ref[first : first + per].reshape(CHUNK, mine_ref.shape[2])
        half = coef_mine[:, first * 128 : first * 128 + CHUNK]
        cot = cot + jnp.dot(half, text, preferred_element_type=F32)
    cot_ref[...] = cot
    sums_ref[...] = before_sums[...] + sums


def cross_kernel(
    scalars_ref,
    image_ref,
    image_far_ref,
    own_sib,
    mine_ref,
    sib_ref,
    before_sums,
    coef_mine,
    cot_ref,
    sums_ref,
    image_out,
    text_sib,
    coef_sib,
):
    image = unit(image_far_ref[...])
    image_out[...] = image
    cot, sums = pairs(scalars_ref, image, sib_ref, coef_sib)
    count = text_sib.shape[0] // 128
    for k in range(count):
        text_sib[k * 128 : (k + 1) * 128] = text_part(own_sib, coef_sib, image_ref, image_out, k).astype(BF16)
    more_cot, more_sums = pairs(scalars_ref, image, mine_ref, coef_mine)
    cot_ref[...] = (cot + more_cot).astype(BF16)
    rest = before_sums[...] + sums + more_sums
    sums_ref[...] = rest
    for term in range(3):
        value = rest.astype(BF16)
        rest = rest - value.astype(F32)
        for k in range(3):
            at = (term * 3 + k) * 128
            text_sib[count * 128 :, at : at + 128] = value[k * PART : (k + 1) * PART]


def text_part(own_ref, cross_ref, image_ref, image_far_ref, block):
    cols = pl.ds(pl.multiple_of(block * 128, 128), 128)
    dims = (((0,), (0,)), ((), ()))
    return lax.dot_general(own_ref[:, cols], image_ref[...], dims, preferred_element_type=F32) + lax.dot_general(
        cross_ref[:, cols], image_far_ref[...], dims, preferred_element_type=F32
    )


def text_mine_kernel(y_ref, own_ref, cross_ref, image_ref, image_far_ref, got_ref, sums_ref, spread_ref, *out_refs):
    count = len(out_refs)
    for k in range(3):
        total = sums_ref[k * PART : (k + 1) * PART]
        for term in range(3):
            at = (term * 3 + k) * 128
            total = total + got_ref[count * 128 :, at : at + 128].astype(F32)
        for peer in range(spread_ref.shape[0]):
            spread_ref[peer, k * PART : (k + 1) * PART] = total
    for k in range(count):
        block = lax.rem(y_ref[0] + k, count)
        total = text_part(own_ref, cross_ref, image_ref, image_far_ref, block) + got_ref[pl.ds(pl.multiple_of(block * 128, 128), 128), :].astype(F32)
        out_refs[k][...] = total.astype(out_refs[k].dtype)


def sum_kernel(near_ref, spread_ref):
    near = jnp.sum(near_ref[...], axis=0)
    lane = lax.broadcasted_iota(jnp.int32, (1, 128), 1)
    row = jnp.zeros((1, 128), F32)
    for k in range(3):
        row = row + jnp.where(lane == k, jnp.sum(near[k * PART : (k + 1) * PART]), 0.0)
    spread_ref[...] = jnp.broadcast_to(row[None], spread_ref.shape)


def pull(embeds, cot, temper):
    floats = embeds.astype(F32)
    cot = temper * cot
    inverse = lax.rsqrt(jnp.sum(floats * floats, axis=1, keepdims=True) + EPSILON)
    along = jnp.sum(cot * floats, axis=1, keepdims=True)
    return (inverse * cot - (inverse * inverse * inverse * along) * floats).astype(BF16)


def grad_kernel(scalars_ref, embeds_ref, cot_ref, *refs):
    cot = cot_ref[...]
    for got_ref in refs[:-1]:
        cot = cot + got_ref[...].astype(F32)
    refs[-1][...] = pull(embeds_ref[...], cot, scalars_ref[0:1, 0:1])


def last_kernel(batch, scalars_ref, embeds_ref, cot_ref, got_ref, totals_ref, grad_ref, loss_ref, scale_grad, bias_grad):
    grad_kernel(scalars_ref, embeds_ref, cot_ref, got_ref, grad_ref)
    totals = jnp.sum(totals_ref[...], axis=0)
    lane = lax.broadcasted_iota(jnp.int32, (1, 128), 1)
    loss, scale, bias = (jnp.sum(jnp.where(lane == k, totals, 0.0)) for k in range(3))
    loss_ref[0] = loss / batch
    scale_grad[0] = scale
    bias_grad[0] = bias


def region(body, inside, *args):
    outs = jax.eval_shape(body, *args)
    return lax.cond(inside, body, lambda *_: jax.tree.map(lambda o: jnp.zeros(o.shape, o.dtype), outs), *args)


def on_device(image_embeds, text_embeds, log_scale, logit_bias):
    rows, width = image_embeds.shape
    y_count = lax.axis_size("y")
    y = jnp.reshape(lax.axis_index("y"), (1,))
    inside = y[0] < y_count
    block, blocks = (rows, width), (y_count, rows, width)
    half = (rows, y_count * rows)

    image_far = lax.ppermute(image_embeds, "zh", SWAP)
    def own_pairs(text_embeds, image_embeds, log_scale, logit_bias, y):
        (text,) = call(norm_kernel, [(blocks, BF16)], [VMEM], (text_embeds,))
        (scalars,) = call(scalars_kernel, [((8, 128), F32)], [SMEM] * 2, (log_scale, logit_bias))
        mine = lax.all_to_all(text, "y", 0, 0, tiled=True)
        sib = lax.ppermute(mine, "c", SWAP)
        coef, sums, image, mine = call(
            own_mine_kernel,
            [(half, BF16), ((3 * PART, 128), F32), (block, BF16), (blocks, BF16)],
            [VMEM, SMEM, VMEM, VMEM],
            (scalars, y, image_embeds, mine),
        )
        return mine, sib, coef, sums, image, scalars

    mine, sib, own_mine, sums, image, scalars = region(
        own_pairs, inside, text_embeds, image_embeds, log_scale, logit_bias, y
    )
    own_sib, image_cot, sums, sib, scalars = call(
        own_sib_kernel,
        [(half, BF16), (block, F32), ((3 * PART, 128), F32), (blocks, BF16), ((8, 128), F32)],
        [VMEM] * 6,
        (scalars, image, sib, mine, own_mine, sums),
    )
    far_mine, far_cot, sums, image_far, text_sib = call(
        cross_kernel,
        [
            (half, BF16),
            (block, BF16),
            ((3 * PART, 128), F32),
            (block, BF16),
            ((y_count * rows + PART, width), BF16),
        ],
        [VMEM] * 7,
        (scalars, image, image_far, own_sib, mine, sib, sums),
        [pltpu.VMEM(half, BF16)],
    )
    far_got = lax.ppermute(far_cot, "zh", SWAP)

    text_got = lax.ppermute(text_sib, "c", SWAP)

    def text_side(own_mine, far_mine, image, image_far, text_got, y, sums, text_embeds, scalars):
        near_axes = ("y", "x")
        spread, text_kept, *text_send = call(
            text_mine_kernel,
            [((lax.axis_size(near_axes), 3 * PART, 128), F32), (block, F32)] + [(block, BF16)] * (y_count - 1),
            [SMEM] + [VMEM] * 6,
            (y, own_mine, far_mine, image, image_far, text_got, sums),
        )
        near = lax.all_to_all(spread, near_axes, 0, 0, tiled=True)
        got = [
            lax.ppermute(part, "y", [(i, (i + k) % y_count) for i in range(y_count)])
            for k, part in enumerate(text_send, 1)
        ]
        z_axes = ("zh", "zl")
        (spread,) = call(sum_kernel, [((lax.axis_size(z_axes), 1, 128), F32)], [VMEM], (near,))
        totals = lax.all_to_all(spread, z_axes, 0, 0, tiled=True)
        (text_grad,) = call(
            grad_kernel,
            [(block, BF16)],
            [VMEM] * (3 + len(got)),
            (scalars, text_embeds, text_kept, *got),
        )
        return text_grad, totals

    text_grad, totals = region(
        text_side,
        inside,
        own_mine,
        far_mine,
        image,
        image_far,
        text_got,
        y,
        sums,
        text_embeds,
        scalars,
    )
    image_grad, loss, scale_grad, bias_grad = call(
        functools.partial(last_kernel, rows * lax.axis_size(AXES)),
        [(block, BF16)] + [((1,), F32)] * 3,
        [VMEM] * 5,
        (scalars, image_embeds, image_cot, far_got, totals),
        out_specs=[VMEM] + [SMEM] * 3,
    )
    return loss, image_grad, text_grad, scale_grad, bias_grad


def solution(mesh):
    fine = Mesh(mesh.devices.reshape(SIZES), AXES)
    return jax.shard_map(
        on_device,
        mesh=fine,
        in_specs=(P(AXES, None), P(AXES, None), P(), P()),
        out_specs=(P(), P(AXES, None), P(AXES, None), P(), P()),
        check_vma=False,
    )
```

```python
import functools

import jax
import jax.numpy as jnp
from jax import lax
from jax.experimental import pallas as pl
from jax.experimental.pallas import tpu as pltpu
from jax.sharding import Mesh, PartitionSpec as P

EPSILON = 1e-06
F32 = jnp.float32
BF16 = jnp.bfloat16
AXES = ("zh", "y", "c", "zl", "x")
SIZES = (2, 4, 2, 8, 4)

VMEM = pl.BlockSpec(memory_space=pltpu.VMEM)
SMEM = pl.BlockSpec(memory_space=pltpu.SMEM)
PARAMS = pltpu.CompilerParams(vmem_limit_bytes=16 * 1024 * 1024)
SWAP = ((0, 1), (1, 0))
CHUNK = 256
PART = 16


def call(kernel, outs, in_specs, args, scratch=(), out_specs=None):
    return pl.pallas_call(
        kernel,
        out_shape=[jax.ShapeDtypeStruct(shape, dtype) for shape, dtype in outs],
        in_specs=in_specs,
        out_specs=out_specs or [VMEM] * len(outs),
        scratch_shapes=scratch,
        compiler_params=PARAMS,
    )(*args)


def unit(matrix):
    floats = matrix.astype(F32)
    return (floats * lax.rsqrt(jnp.sum(floats * floats, axis=1, keepdims=True) + EPSILON)).astype(BF16)


def norm_kernel(matrix_ref, out_ref):
    rows = unit(matrix_ref[...])
    for k in range(out_ref.shape[0]):
        out_ref[k] = rows


def scalars_kernel(scale_ref, bias_ref, scalars_ref):
    row = lax.broadcasted_iota(jnp.int32, scalars_ref.shape, 0)
    temper = jnp.exp(jnp.full(scalars_ref.shape, scale_ref[0], F32))
    scalars_ref[...] = jnp.where(row == 0, temper, bias_ref[0])


def lanes(values):
    return sum(values[:, k * 128 : (k + 1) * 128] for k in range(values.shape[1] // 128))


def fold(values):
    rows, cols = values.shape
    return lanes(jnp.sum(values.reshape(rows // PART, PART, cols), axis=0))


def fold_logs(values):
    rows, cols = values.shape
    parts = values.reshape(rows // PART, PART, cols)
    while parts.shape[0] > 1:
        middle = parts.shape[0] // 2
        parts = parts[:middle] * parts[middle:]
    return lanes(jnp.log(parts[0]))


def pair_chunk(image, text, temper, offset, positive):
    products = lax.dot_general(image, text, (((1,), (1,)), ((), ())), preferred_element_type=F32)
    scaled = temper * products
    logits = scaled + offset
    small = jnp.exp(-jnp.abs(logits))
    part = 1.0 / (1.0 + small)
    coef = jnp.where(logits >= 0.0, 1.0, small) * part
    signed = logits
    if positive is not None:
        coef = coef - jnp.where(positive, 1.0, 0.0)
        signed = jnp.where(positive, -logits, logits)
    loss = fold(jnp.maximum(signed, 0.0)) + fold_logs(1.0 + small)
    return coef, (loss, fold(coef * scaled), fold(coef))


def pairs(scalars_ref, image, text_ref, coef_ref, y=None, pull_back=True):
    per = CHUNK // 128
    temper = scalars_ref[0:1, 0:1]
    offset = scalars_ref[1:2, 0:1]
    sums, cot = None, None
    for first in range(0, text_ref.shape[0], per):
        text = text_ref[first : first + per].reshape(CHUNK, text_ref.shape[2])
        positive = None
        if y is not None:
            rows = lax.broadcasted_iota(jnp.int32, (128, CHUNK), 0)
            cols = lax.broadcasted_iota(jnp.int32, (128, CHUNK), 1)
            positive = cols + first * 128 == rows + y * 128
        coef, terms = pair_chunk(image, text, temper, offset, positive)
        half = coef.astype(BF16)
        coef_ref[:, first * 128 : first * 128 + CHUNK] = half
        if pull_back:
            part = jnp.dot(half, text, preferred_element_type=F32)
            cot = part if cot is None else cot + part
        sums = terms if sums is None else tuple(a + b for a, b in zip(sums, terms))
    return cot, jnp.concatenate(sums, axis=0)


def own_mine_kernel(
    scalars_ref, y_ref, image_ref, text_ref, coef_ref, sums_ref, image_out, text_out
):
    text_out[...] = text_ref[...]
    image = unit(image_ref[...])
    image_out[...] = image
    _, sums_ref[...] = pairs(scalars_ref, image, text_ref, coef_ref, y_ref[0], False)


def own_sib_kernel(
    scalars_ref,
    image_ref,
    sib_ref,
    mine_ref,
    coef_mine,
    before_sums,
    coef_ref,
    cot_ref,
    sums_ref,
    sib_out,
    scalars_out,
):
    scalars_out[...] = scalars_ref[...]
    sib_out[...] = sib_ref[...]
    cot, sums = pairs(scalars_ref, image_ref[...], sib_ref, coef_ref)
    per = CHUNK // 128
    for first in range(0, mine_ref.shape[0], per):
        text = mine_ref[first : first + per].reshape(CHUNK, mine_ref.shape[2])
        half = coef_mine[:, first * 128 : first * 128 + CHUNK]
        cot = cot + jnp.dot(half, text, preferred_element_type=F32)
    cot_ref[...] = cot
    sums_ref[...] = before_sums[...] + sums


def cross_kernel(
    scalars_ref,
    image_ref,
    image_far_ref,
    own_sib,
    mine_ref,
    sib_ref,
    before_sums,
    coef_mine,
    cot_ref,
    sums_ref,
    image_out,
    text_sib,
    coef_sib,
):
    image = unit(image_far_ref[...])
    image_out[...] = image
    cot, sums = pairs(scalars_ref, image, sib_ref, coef_sib)
    count = text_sib.shape[0] // 128
    for k in range(count):
        text_sib[k * 128 : (k + 1) * 128] = text_part(own_sib, coef_sib, image_ref, image_out, k).astype(BF16)
    more_cot, more_sums = pairs(scalars_ref, image, mine_ref, coef_mine)
    cot_ref[...] = (cot + more_cot).astype(BF16)
    rest = before_sums[...] + sums + more_sums
    sums_ref[...] = rest
    for term in range(3):
        value = rest.astype(BF16)
        rest = rest - value.astype(F32)
        for k in range(3):
            at = (term * 3 + k) * 128
            text_sib[count * 128 :, at : at + 128] = value[k * PART : (k + 1) * PART]


def text_part(own_ref, cross_ref, image_ref, image_far_ref, block):
    cols = pl.ds(pl.multiple_of(block * 128, 128), 128)
    dims = (((0,), (0,)), ((), ()))
    return lax.dot_general(own_ref[:, cols], image_ref[...], dims, preferred_element_type=F32) + lax.dot_general(
        cross_ref[:, cols], image_far_ref[...], dims, preferred_element_type=F32
    )


def text_mine_kernel(y_ref, own_ref, cross_ref, image_ref, image_far_ref, got_ref, sums_ref, spread_ref, *out_refs):
    count = len(out_refs)
    for k in range(3):
        total = sums_ref[k * PART : (k + 1) * PART]
        for term in range(3):
            at = (term * 3 + k) * 128
            total = total + got_ref[count * 128 :, at : at + 128].astype(F32)
        for peer in range(spread_ref.shape[0]):
            spread_ref[peer, k * PART : (k + 1) * PART] = total
    for k in range(count):
        block = lax.rem(y_ref[0] + k, count)
        total = text_part(own_ref, cross_ref, image_ref, image_far_ref, block) + got_ref[pl.ds(pl.multiple_of(block * 128, 128), 128), :].astype(F32)
        out_refs[k][...] = total.astype(out_refs[k].dtype)


def sum_kernel(near_ref, spread_ref):
    near = jnp.sum(near_ref[...], axis=0)
    lane = lax.broadcasted_iota(jnp.int32, (1, 128), 1)
    row = jnp.zeros((1, 128), F32)
    for k in range(3):
        row = row + jnp.where(lane == k, jnp.sum(near[k * PART : (k + 1) * PART]), 0.0)
    spread_ref[...] = jnp.broadcast_to(row[None], spread_ref.shape)


def pull(embeds, cot, temper):
    floats = embeds.astype(F32)
    cot = temper * cot
    inverse = lax.rsqrt(jnp.sum(floats * floats, axis=1, keepdims=True) + EPSILON)
    along = jnp.sum(cot * floats, axis=1, keepdims=True)
    return (inverse * cot - (inverse * inverse * inverse * along) * floats).astype(BF16)


def grad_kernel(scalars_ref, embeds_ref, cot_ref, *refs):
    cot = cot_ref[...]
    for got_ref in refs[:-1]:
        cot = cot + got_ref[...].astype(F32)
    refs[-1][...] = pull(embeds_ref[...], cot, scalars_ref[0:1, 0:1])


def last_kernel(batch, scalars_ref, embeds_ref, cot_ref, got_ref, totals_ref, grad_ref, loss_ref, scale_grad, bias_grad):
    grad_kernel(scalars_ref, embeds_ref, cot_ref, got_ref, grad_ref)
    totals = jnp.sum(totals_ref[...], axis=0)
    lane = lax.broadcasted_iota(jnp.int32, (1, 128), 1)
    loss, scale, bias = (jnp.sum(jnp.where(lane == k, totals, 0.0)) for k in range(3))
    loss_ref[0] = loss / batch
    scale_grad[0] = scale
    bias_grad[0] = bias


def region(body, inside, *args):
    outs = jax.eval_shape(body, *args)
    return lax.cond(inside, body, lambda *_: jax.tree.map(lambda o: jnp.zeros(o.shape, o.dtype), outs), *args)


def on_device(image_embeds, text_embeds, log_scale, logit_bias):
    rows, width = image_embeds.shape
    y_count = lax.axis_size("y")
    y = jnp.reshape(lax.axis_index("y"), (1,))
    inside = y[0] < y_count
    block, blocks = (rows, width), (y_count, rows, width)
    half = (rows, y_count * rows)

    image_far = lax.ppermute(image_embeds, "zh", SWAP)
    def own_pairs(text_embeds, image_embeds, log_scale, logit_bias, y):
        (text,) = call(norm_kernel, [(blocks, BF16)], [VMEM], (text_embeds,))
        (scalars,) = call(scalars_kernel, [((8, 128), F32)], [SMEM] * 2, (log_scale, logit_bias))
        mine = lax.all_to_all(text, "y", 0, 0, tiled=True)
        sib = lax.ppermute(mine, "c", SWAP)
        coef, sums, image, mine = call(
            own_mine_kernel,
            [(half, BF16), ((3 * PART, 128), F32), (block, BF16), (blocks, BF16)],
            [VMEM, SMEM, VMEM, VMEM],
            (scalars, y, image_embeds, mine),
        )
        return mine, sib, coef, sums, image, scalars

    mine, sib, own_mine, sums, image, scalars = region(
        own_pairs, inside, text_embeds, image_embeds, log_scale, logit_bias, y
    )
    own_sib, image_cot, sums, sib, scalars = call(
        own_sib_kernel,
        [(half, BF16), (block, F32), ((3 * PART, 128), F32), (blocks, BF16), ((8, 128), F32)],
        [VMEM] * 6,
        (scalars, image, sib, mine, own_mine, sums),
    )
    far_mine, far_cot, sums, image_far, text_sib = call(
        cross_kernel,
        [
            (half, BF16),
            (block, BF16),
            ((3 * PART, 128), F32),
            (block, BF16),
            ((y_count * rows + PART, width), BF16),
        ],
        [VMEM] * 7,
        (scalars, image, image_far, own_sib, mine, sib, sums),
        [pltpu.VMEM(half, BF16)],
    )
    far_got = lax.ppermute(far_cot, "zh", SWAP)

    text_got = lax.ppermute(text_sib, "c", SWAP)

    def text_side(own_mine, far_mine, image, image_far, text_got, y, sums, text_embeds, scalars):
        near_axes = ("y", "x")
        spread, text_kept, *text_send = call(
            text_mine_kernel,
            [((lax.axis_size(near_axes), 3 * PART, 128), F32), (block, F32)] + [(block, BF16)] * (y_count - 1),
            [SMEM] + [VMEM] * 6,
            (y, own_mine, far_mine, image, image_far, text_got, sums),
        )
        near = lax.all_to_all(spread, near_axes, 0, 0, tiled=True)
        def shift(k):
            return lambda part: lax.ppermute(part, "y", [(i, (i + k) % y_count) for i in range(y_count)])

        order = sorted(range(1, y_count), key=lambda k: -min(k, y_count - k))
        got = [shift(k)(text_send[k - 1]) for k in order[:-1]]
        z_axes = ("zh", "zl")
        (spread,) = call(sum_kernel, [((lax.axis_size(z_axes), 1, 128), F32)], [VMEM], (near,))
        totals = lax.all_to_all(spread, z_axes, 0, 0, tiled=True)
        got.append(region(shift(order[-1]), y[0] < y_count, text_send[order[-1] - 1]))
        (text_grad,) = call(
            grad_kernel,
            [(block, BF16)],
            [VMEM] * (3 + len(got)),
            (scalars, text_embeds, text_kept, *got),
        )
        return text_grad, totals

    text_grad, totals = region(
        text_side,
        inside,
        own_mine,
        far_mine,
        image,
        image_far,
        text_got,
        y,
        sums,
        text_embeds,
        scalars,
    )
    image_grad, loss, scale_grad, bias_grad = call(
        functools.partial(last_kernel, rows * lax.axis_size(AXES)),
        [(block, BF16)] + [((1,), F32)] * 3,
        [VMEM] * 5,
        (scalars, image_embeds, image_cot, far_got, totals),
        out_specs=[VMEM] + [SMEM] * 3,
    )
    return loss, image_grad, text_grad, scale_grad, bias_grad


def solution(mesh):
    fine = Mesh(mesh.devices.reshape(SIZES), AXES)
    return jax.shard_map(
        on_device,
        mesh=fine,
        in_specs=(P(AXES, None), P(AXES, None), P(), P()),
        out_specs=(P(), P(AXES, None), P(AXES, None), P(), P()),
        check_vma=False,
    )
```

```python
import functools

import jax
import jax.numpy as jnp
from jax import lax
from jax.experimental import pallas as pl
from jax.experimental.pallas import tpu as pltpu
from jax.sharding import Mesh, PartitionSpec as P

EPSILON = 1e-06
F32 = jnp.float32
BF16 = jnp.bfloat16
AXES = ("zh", "y", "c", "zl", "x")
SIZES = (2, 4, 2, 8, 4)

VMEM = pl.BlockSpec(memory_space=pltpu.VMEM)
SMEM = pl.BlockSpec(memory_space=pltpu.SMEM)
PARAMS = pltpu.CompilerParams(vmem_limit_bytes=16 * 1024 * 1024)
SWAP = ((0, 1), (1, 0))
CHUNK = 512
PART = 16


def call(kernel, outs, in_specs, args, scratch=(), out_specs=None):
    return pl.pallas_call(
        kernel,
        out_shape=[jax.ShapeDtypeStruct(shape, dtype) for shape, dtype in outs],
        in_specs=in_specs,
        out_specs=out_specs or [VMEM] * len(outs),
        scratch_shapes=scratch,
        compiler_params=PARAMS,
    )(*args)


def unit(matrix):
    floats = matrix.astype(F32)
    return (floats * lax.rsqrt(jnp.sum(floats * floats, axis=1, keepdims=True) + EPSILON)).astype(BF16)


def norm_kernel(matrix_ref, out_ref):
    rows = unit(matrix_ref[...])
    for k in range(out_ref.shape[0]):
        out_ref[k] = rows


def scalars_kernel(scale_ref, bias_ref, scalars_ref):
    row = lax.broadcasted_iota(jnp.int32, scalars_ref.shape, 0)
    temper = jnp.exp(jnp.full(scalars_ref.shape, scale_ref[0], F32))
    scalars_ref[...] = jnp.where(row == 0, temper, bias_ref[0])


def lanes(values):
    return sum(values[:, k * 128 : (k + 1) * 128] for k in range(values.shape[1] // 128))


def fold(values):
    rows, cols = values.shape
    return lanes(jnp.sum(values.reshape(rows // PART, PART, cols), axis=0))


def fold_logs(values):
    rows, cols = values.shape
    parts = values.reshape(rows // PART, PART, cols)
    while parts.shape[0] > 1:
        middle = parts.shape[0] // 2
        parts = parts[:middle] * parts[middle:]
    return lanes(jnp.log(parts[0]))


def pair_chunk(image, text, temper, offset, positive):
    products = lax.dot_general(image, text, (((1,), (1,)), ((), ())), preferred_element_type=F32)
    scaled = temper * products
    logits = scaled + offset
    small = jnp.exp(-jnp.abs(logits))
    part = 1.0 / (1.0 + small)
    coef = jnp.where(logits >= 0.0, 1.0, small) * part
    signed = logits
    if positive is not None:
        coef = coef - jnp.where(positive, 1.0, 0.0)
        signed = jnp.where(positive, -logits, logits)
    loss = fold(jnp.maximum(signed, 0.0)) + fold_logs(1.0 + small)
    return coef, (loss, fold(coef * scaled), fold(coef))


def pairs(scalars_ref, image, text_ref, coef_ref, y=None, pull_back=True):
    per = CHUNK // 128
    temper = scalars_ref[0:1, 0:1]
    offset = scalars_ref[1:2, 0:1]
    sums, cot = None, None
    for first in range(0, text_ref.shape[0], per):
        text = text_ref[first : first + per].reshape(CHUNK, text_ref.shape[2])
        positive = None
        if y is not None:
            rows = lax.broadcasted_iota(jnp.int32, (128, CHUNK), 0)
            cols = lax.broadcasted_iota(jnp.int32, (128, CHUNK), 1)
            positive = cols + first * 128 == rows + y * 128
        coef, terms = pair_chunk(image, text, temper, offset, positive)
        half = coef.astype(BF16)
        coef_ref[:, first * 128 : first * 128 + CHUNK] = half
        if pull_back:
            part = jnp.dot(half, text, preferred_element_type=F32)
            cot = part if cot is None else cot + part
        sums = terms if sums is None else tuple(a + b for a, b in zip(sums, terms))
    return cot, jnp.concatenate(sums, axis=0)


def own_mine_kernel(
    scalars_ref, y_ref, image_ref, text_ref, coef_ref, sums_ref, image_out, text_out
):
    text_out[...] = text_ref[...]
    image = unit(image_ref[...])
    image_out[...] = image
    _, sums_ref[...] = pairs(scalars_ref, image, text_ref, coef_ref, y_ref[0], False)


def own_sib_kernel(
    scalars_ref,
    image_ref,
    sib_ref,
    mine_ref,
    coef_mine,
    before_sums,
    coef_ref,
    cot_ref,
    sums_ref,
    sib_out,
    scalars_out,
):
    scalars_out[...] = scalars_ref[...]
    sib_out[...] = sib_ref[...]
    cot, sums = pairs(scalars_ref, image_ref[...], sib_ref, coef_ref)
    per = CHUNK // 128
    for first in range(0, mine_ref.shape[0], per):
        text = mine_ref[first : first + per].reshape(CHUNK, mine_ref.shape[2])
        half = coef_mine[:, first * 128 : first * 128 + CHUNK]
        cot = cot + jnp.dot(half, text, preferred_element_type=F32)
    cot_ref[...] = cot
    sums_ref[...] = before_sums[...] + sums


def cross_kernel(
    scalars_ref,
    image_ref,
    image_far_ref,
    own_sib,
    mine_ref,
    sib_ref,
    before_sums,
    coef_mine,
    cot_ref,
    sums_ref,
    image_out,
    text_sib,
    coef_sib,
):
    image = unit(image_far_ref[...])
    image_out[...] = image
    cot, sums = pairs(scalars_ref, image, sib_ref, coef_sib)
    count = text_sib.shape[0] // 128
    for k in range(count):
        text_sib[k * 128 : (k + 1) * 128] = text_part(own_sib, coef_sib, image_ref, image_out, k).astype(BF16)
    more_cot, more_sums = pairs(scalars_ref, image, mine_ref, coef_mine)
    cot_ref[...] = (cot + more_cot).astype(BF16)
    rest = before_sums[...] + sums + more_sums
    sums_ref[...] = rest
    for term in range(3):
        value = rest.astype(BF16)
        rest = rest - value.astype(F32)
        for k in range(3):
            at = (term * 3 + k) * 128
            text_sib[count * 128 :, at : at + 128] = value[k * PART : (k + 1) * PART]


def text_part(own_ref, cross_ref, image_ref, image_far_ref, block):
    cols = pl.ds(pl.multiple_of(block * 128, 128), 128)
    dims = (((0,), (0,)), ((), ()))
    return lax.dot_general(own_ref[:, cols], image_ref[...], dims, preferred_element_type=F32) + lax.dot_general(
        cross_ref[:, cols], image_far_ref[...], dims, preferred_element_type=F32
    )


def text_mine_kernel(y_ref, own_ref, cross_ref, image_ref, image_far_ref, got_ref, sums_ref, spread_ref, *out_refs):
    count = len(out_refs)
    for k in range(3):
        total = sums_ref[k * PART : (k + 1) * PART]
        for term in range(3):
            at = (term * 3 + k) * 128
            total = total + got_ref[count * 128 :, at : at + 128].astype(F32)
        for peer in range(spread_ref.shape[0]):
            spread_ref[peer, k * PART : (k + 1) * PART] = total
    for k in range(count):
        block = lax.rem(y_ref[0] + k, count)
        total = text_part(own_ref, cross_ref, image_ref, image_far_ref, block) + got_ref[pl.ds(pl.multiple_of(block * 128, 128), 128), :].astype(F32)
        out_refs[k][...] = total.astype(out_refs[k].dtype)


def sum_kernel(near_ref, spread_ref):
    near = jnp.sum(near_ref[...], axis=0)
    lane = lax.broadcasted_iota(jnp.int32, (1, 128), 1)
    row = jnp.zeros((1, 128), F32)
    for k in range(3):
        row = row + jnp.where(lane == k, jnp.sum(near[k * PART : (k + 1) * PART]), 0.0)
    spread_ref[...] = jnp.broadcast_to(row[None], spread_ref.shape)


def pull(embeds, cot, temper):
    floats = embeds.astype(F32)
    cot = temper * cot
    inverse = lax.rsqrt(jnp.sum(floats * floats, axis=1, keepdims=True) + EPSILON)
    along = jnp.sum(cot * floats, axis=1, keepdims=True)
    return (inverse * cot - (inverse * inverse * inverse * along) * floats).astype(BF16)


def grad_kernel(scalars_ref, embeds_ref, cot_ref, *refs):
    cot = cot_ref[...]
    for got_ref in refs[:-1]:
        cot = cot + got_ref[...].astype(F32)
    refs[-1][...] = pull(embeds_ref[...], cot, scalars_ref[0:1, 0:1])


def last_kernel(batch, scalars_ref, embeds_ref, cot_ref, got_ref, totals_ref, grad_ref, loss_ref, scale_grad, bias_grad):
    grad_kernel(scalars_ref, embeds_ref, cot_ref, got_ref, grad_ref)
    totals = jnp.sum(totals_ref[...], axis=0)
    lane = lax.broadcasted_iota(jnp.int32, (1, 128), 1)
    loss, scale, bias = (jnp.sum(jnp.where(lane == k, totals, 0.0)) for k in range(3))
    loss_ref[0] = loss / batch
    scale_grad[0] = scale
    bias_grad[0] = bias


def region(body, inside, *args):
    outs = jax.eval_shape(body, *args)
    return lax.cond(inside, body, lambda *_: jax.tree.map(lambda o: jnp.zeros(o.shape, o.dtype), outs), *args)


def on_device(image_embeds, text_embeds, log_scale, logit_bias):
    rows, width = image_embeds.shape
    y_count = lax.axis_size("y")
    y = jnp.reshape(lax.axis_index("y"), (1,))
    inside = y[0] < y_count
    block, blocks = (rows, width), (y_count, rows, width)
    half = (rows, y_count * rows)

    image_far = lax.ppermute(image_embeds, "zh", SWAP)
    def own_pairs(text_embeds, image_embeds, log_scale, logit_bias, y):
        (text,) = call(norm_kernel, [(blocks, BF16)], [VMEM], (text_embeds,))
        (scalars,) = call(scalars_kernel, [((8, 128), F32)], [SMEM] * 2, (log_scale, logit_bias))
        mine = lax.all_to_all(text, "y", 0, 0, tiled=True)
        sib = lax.ppermute(mine, "c", SWAP)
        coef, sums, image, mine = call(
            own_mine_kernel,
            [(half, BF16), ((3 * PART, 128), F32), (block, BF16), (blocks, BF16)],
            [VMEM, SMEM, VMEM, VMEM],
            (scalars, y, image_embeds, mine),
        )
        return mine, sib, coef, sums, image, scalars

    mine, sib, own_mine, sums, image, scalars = region(
        own_pairs, inside, text_embeds, image_embeds, log_scale, logit_bias, y
    )
    own_sib, image_cot, sums, sib, scalars = call(
        own_sib_kernel,
        [(half, BF16), (block, F32), ((3 * PART, 128), F32), (blocks, BF16), ((8, 128), F32)],
        [VMEM] * 6,
        (scalars, image, sib, mine, own_mine, sums),
    )
    far_mine, far_cot, sums, image_far, text_sib = call(
        cross_kernel,
        [
            (half, BF16),
            (block, BF16),
            ((3 * PART, 128), F32),
            (block, BF16),
            ((y_count * rows + PART, width), BF16),
        ],
        [VMEM] * 7,
        (scalars, image, image_far, own_sib, mine, sib, sums),
        [pltpu.VMEM(half, BF16)],
    )
    far_got = lax.ppermute(far_cot, "zh", SWAP)

    text_got = lax.ppermute(text_sib, "c", SWAP)

    def text_side(own_mine, far_mine, image, image_far, text_got, y, sums, text_embeds, scalars):
        near_axes = ("y", "x")
        spread, text_kept, *text_send = call(
            text_mine_kernel,
            [((lax.axis_size(near_axes), 3 * PART, 128), F32), (block, F32)] + [(block, BF16)] * (y_count - 1),
            [SMEM] + [VMEM] * 6,
            (y, own_mine, far_mine, image, image_far, text_got, sums),
        )
        near = lax.all_to_all(spread, near_axes, 0, 0, tiled=True)
        def shift(k):
            return lambda part: lax.ppermute(part, "y", [(i, (i + k) % y_count) for i in range(y_count)])

        order = sorted(range(1, y_count), key=lambda k: -min(k, y_count - k))
        got = [shift(k)(text_send[k - 1]) for k in order[:-1]]
        z_axes = ("zh", "zl")
        (spread,) = call(sum_kernel, [((lax.axis_size(z_axes), 1, 128), F32)], [VMEM], (near,))
        totals = lax.all_to_all(spread, z_axes, 0, 0, tiled=True)
        got.append(region(shift(order[-1]), y[0] < y_count, text_send[order[-1] - 1]))
        (text_grad,) = call(
            grad_kernel,
            [(block, BF16)],
            [VMEM] * (3 + len(got)),
            (scalars, text_embeds, text_kept, *got),
        )
        return text_grad, totals

    text_grad, totals = region(
        text_side,
        inside,
        own_mine,
        far_mine,
        image,
        image_far,
        text_got,
        y,
        sums,
        text_embeds,
        scalars,
    )
    image_grad, loss, scale_grad, bias_grad = call(
        functools.partial(last_kernel, rows * lax.axis_size(AXES)),
        [(block, BF16)] + [((1,), F32)] * 3,
        [VMEM] * 5,
        (scalars, image_embeds, image_cot, far_got, totals),
        out_specs=[VMEM] + [SMEM] * 3,
    )
    return loss, image_grad, text_grad, scale_grad, bias_grad


def solution(mesh):
    fine = Mesh(mesh.devices.reshape(SIZES), AXES)
    return jax.shard_map(
        on_device,
        mesh=fine,
        in_specs=(P(AXES, None), P(AXES, None), P(), P()),
        out_specs=(P(), P(AXES, None), P(AXES, None), P(), P()),
        check_vma=False,
    )
```
